256 devices in a mesh: gx: 4 (over y_lo, core), gy: 4 (over x), gz: 16 (over z, y_hi).
Axes of the slice: x: 4, y: 4 (y_hi: 2, y_lo: 2; y = y_hi * 2 + y_lo), z: 8, core: 2. Of those that a mesh axis runs over, the one named last changes fastest.
Arguments:
- positions: bfloat16 [4, 4, 16, 3, 432], P('gx', 'gy', 'gz'), may hold values from 0 to 15, as said below
- features: bfloat16 [4, 4, 16, 128, 432], P('gx', 'gy', 'gz'), may hold values from -6 to 6
- species: int32 [4, 4, 16, 432], P('gx', 'gy', 'gz'), may hold values from 0 to 9
- species_shift: float32 [10], replicated, may hold values from -4 to 4
- send_index: int32 [4, 4, 16, 304], P('gx', 'gy', 'gz'), may hold values from 0 to 431, as said below
- pair_target: int32 [4, 4, 16, 10, 128], P('gx', 'gy', 'gz'), may hold values from 0 to 431, as said below
- pair_source: int32 [4, 4, 16, 10, 128], P('gx', 'gy', 'gz'), may hold values from 0 to 8639, as said below
- block_count: int32 [4, 4, 16], P('gx', 'gy', 'gz'), may hold values from 3 to 10, as said below
- radial_first: bfloat16 [8, 64], replicated, may hold values from -4 to 4
- radial_second: bfloat16 [64, 64], replicated, may hold values from -1 to 1
- radial_third: bfloat16 [64, 384], replicated, may hold values from -1.5 to 1.5
- invariant_mix: bfloat16 [384, 128], replicated, may hold values from -0.3125 to 0.3125
- energy_head: bfloat16 [128], replicated, may hold values from -1 to 1
Outputs:
- energies: float32 [4, 4, 16, 432], P('gx', 'gy', 'gz')
- forces: float32 [4, 4, 16, 3, 432], P('gx', 'gy', 'gz')
The draws below stay inside these ranges and needn't reach their ends.
Inputs may be any that keep to these rules, and one draw needn't show every extreme that they name: `positions`: the atoms of a slab fill a grid of 6 x 6 x 6 cells of side 2.5, 2 atoms to a cell. `send_index`: each slab's list holds, each once, the atoms of its outer layer of cells. `pair_target`: within a slab no pair of target and source repeats. `pair_source`: the source is never the target and lies in the target's cell or in one of the 26 cells around it; a cell beyond a face of the slab is the neighbouring slab's, and its atom then stands in that slab's slot of the ghost table. `block_count`: some slab uses all 10 blocks in every draw.
All inputs are finite; a program needn't handle non-finite values.
Results may differ from the reference program's by a relative error of at most 0.0006.
Values may be sent and summed in bfloat16 or wider, within the bound.
A program may use at most 64 MiB of HBM per device.

```python
import jax
import jax.numpy as jnp
from jax import lax

CH = 128
RH = 64
NRB = 8
SPECIES = 10
K = 6
PER_CELL = 2
A = 432
G = 304
NB = 10
PB = 128
N_GX = 4
N_GY = 4
N_GZ = 16


cell_side = 2.5


def cell_layout(key):
    slabs = N_GX * N_GY * N_GZ
    slab_keys = jax.random.split(jax.random.fold_in(key, 31), slabs)

    def shuffle_slab(slab_key):
        return jax.random.permutation(slab_key, A)
    atom_at = jax.vmap(shuffle_slab)(slab_keys).astype(jnp.int32)
    slot_of = jnp.argsort(atom_at, axis=1, stable=True).astype(jnp.int32)
    return (atom_at, slot_of)


def boundary_table():
    slot_ids = jnp.arange(A).astype(jnp.int32)
    cell_ids = slot_ids // PER_CELL
    coords = jnp.stack([cell_ids // (K * K), cell_ids // K % K, cell_ids % K], 0)
    on_face = jnp.any((coords == 0) | (coords == K - 1), axis=0)
    border_rank = (jnp.cumsum(on_face.astype(jnp.int32)) - 1).astype(jnp.int32)
    border_slots = jnp.nonzero(on_face, size=G)[0].astype(jnp.int32)
    return (border_rank, border_slots)


def cross_axis(coord, offset):
    shifted = coord + offset - 1
    crossing = (shifted >= K).astype(jnp.int32) - (shifted < 0).astype(jnp.int32)
    return (shifted - crossing * K, crossing)


def pair_layout(key):
    atom_at, slot_of = cell_layout(key)
    border_rank, border_slots = boundary_table()
    slabs = N_GX * N_GY * N_GZ
    reach = 27 * PER_CELL - 1
    slab_keys = jax.random.split(jax.random.fold_in(key, 101), slabs)

    def pick_order(slab_key):
        return jax.random.permutation(slab_key, A * reach)[:NB * PB]
    picked = jax.vmap(pick_order)(slab_keys).astype(jnp.int32)
    target_atom = picked // reach
    within = picked % reach
    target_slot = jnp.take_along_axis(slot_of, target_atom, axis=1)
    own_sub = target_slot % PER_CELL
    within = within + (within >= 13 * PER_CELL + own_sub).astype(jnp.int32)
    neighbour_cell = within // PER_CELL
    neighbour_sub = within % PER_CELL
    target_cell = target_slot // PER_CELL
    coord_x, cross_x = cross_axis(target_cell // (K * K), neighbour_cell // 9)
    coord_y, cross_y = cross_axis(target_cell // K % K, neighbour_cell // 3 % 3)
    coord_z, cross_z = cross_axis(target_cell % K, neighbour_cell % 3)
    source_slot = ((coord_x * K + coord_y) * K + coord_z) * PER_CELL + neighbour_sub
    ghost_slot = 9 * (cross_x + 1) + 3 * (cross_y + 1) + cross_z + 1
    owned_atom = jnp.take_along_axis(atom_at, source_slot, axis=1)
    ghost_index = A + ghost_slot * G + jnp.take(border_rank, source_slot)
    source = jnp.where(ghost_slot == 13, owned_atom, ghost_index)
    layout = (N_GX, N_GY, N_GZ, NB, PB)
    return (target_atom.reshape(layout).astype(jnp.int32), source.reshape(layout).astype(jnp.int32))


def draw_positions(key, part):
    atom_at, slot_of = cell_layout(key)
    key = jax.random.fold_in(key, 3)
    slabs = N_GX * N_GY * N_GZ
    cell_ids = slot_of // PER_CELL
    coords = jnp.stack([cell_ids // (K * K), cell_ids // K % K, cell_ids % K], 1).astype(jnp.float32)
    jitter = jax.random.uniform(key, (slabs, 3, A), jnp.float32, -0.35, 0.35)
    placed = (coords + 0.5 + jitter) * cell_side
    return placed.reshape(N_GX, N_GY, N_GZ, 3, A).astype(jnp.bfloat16)


def draw_send_index(key, part):
    atom_at, slot_of = cell_layout(key)
    key = jax.random.fold_in(key, 5)
    border_rank, border_slots = boundary_table()
    listed = jnp.take(atom_at, border_slots, axis=1)
    return listed.reshape(N_GX, N_GY, N_GZ, G).astype(jnp.int32)


def draw_pair_target(key, part):
    targets, sources = pair_layout(key)
    key = jax.random.fold_in(key, 9)
    return targets


def draw_pair_source(key, part):
    targets, sources = pair_layout(key)
    key = jax.random.fold_in(key, 13)
    return sources


def draw_block_count(key, part):
    key = jax.random.fold_in(key, 7)
    first_key, second_key = jax.random.split(key)
    slabs = N_GX * N_GY * N_GZ
    counts = jax.random.randint(first_key, (slabs,), NB // 3, NB + 1)
    busiest = jax.random.randint(second_key, (), 0, slabs)
    counts = jnp.where(jnp.arange(slabs) == busiest, NB, counts)
    return counts.reshape(N_GX, N_GY, N_GZ).astype(jnp.int32)


def plant(drawn, stream_key, least, high):
    longest = drawn.shape.index(max(drawn.shape))
    spots = []
    for shift in (0, 1):
        where = [jax.random.randint(jax.random.fold_in(stream_key, axis), (), 0, length) for axis, length in enumerate(drawn.shape)]
        where[longest] = (where[longest] + shift) % drawn.shape[longest]
        spots.append(tuple(where))
    return drawn.at[spots[0]].set(least).at[spots[1]].set(high)


def steps_of(own_key, extent, pieces, low, top_value):
    factor_of, own = 1.0, jax.random.fold_in(own_key, 6)
    for axis_at, shards_of in pieces:
        steps = jnp.exp(jax.random.uniform(jax.random.fold_in(own, axis_at), (shards_of,), jnp.float32, low / len(pieces), top_value / len(pieces)))
        factor_of = factor_of * jnp.repeat(steps, extent[axis_at] // shards_of).reshape([-1 if axis == axis_at else 1 for axis in range(len(extent))])
    return factor_of


def noise(own_key, extent, scale, most, cuts=(), held_as=jnp.bfloat16):
    drawn = jax.random.normal(own_key, extent, jnp.float32) * scale
    if len(cuts) > 0:
        drawn = steps_of(own_key, extent, cuts, -0.22, 0.18) * drawn
    return jnp.clip(drawn, min=-most, max=most).astype(held_as)


def setup_inputs(seed: int = 0) -> dict:
    splits = jax.random.split(jax.random.key(seed), 14)
    positions = draw_positions(jax.random.fold_in(splits[13], 71), 0)
    features = noise(splits[1], (N_GX, N_GY, N_GZ, CH, A), 1.0, 6.0, ((0, 4), (1, 4), (2, 16)))
    species = plant(jax.random.randint(splits[2], (N_GX, N_GY, N_GZ, A), 0, SPECIES), jax.random.fold_in(splits[2], 1), 0, SPECIES - 1).astype(jnp.int32)
    species_shift = noise(splits[3], (SPECIES,), 1.0, 4.0, (), jnp.float32)
    send_index = draw_send_index(jax.random.fold_in(splits[13], 71), 0)
    pair_target = draw_pair_target(jax.random.fold_in(splits[13], 71), 0)
    pair_source = draw_pair_source(jax.random.fold_in(splits[13], 71), 0)
    block_count = draw_block_count(jax.random.fold_in(splits[13], 71), 0)
    radial_first = noise(splits[8], (NRB, RH), (NRB // 4) ** -0.5, 4.0)
    radial_second = noise(splits[9], (RH, RH), (RH // 2) ** -0.5, 1.0)
    radial_third = noise(splits[10], (RH, 3 * CH), (RH // 4) ** -0.5, 1.5)
    invariant_mix = noise(splits[11], (3 * CH, CH), (3 * CH) ** -0.5, 0.3125)
    energy_head = noise(splits[12], (CH,), (CH // 4) ** -0.5, 1.0)
    return dict(positions=positions, features=features, species=species, species_shift=species_shift, send_index=send_index, pair_target=pair_target, pair_source=pair_source, block_count=block_count, radial_first=radial_first, radial_second=radial_second, radial_third=radial_third, invariant_mix=invariant_mix, energy_head=energy_head)


cutoff_square = 25.0
basis_width = 25.0
cell_side = 2.5
message_scale = 0.15
root_three = 1.7320508075688772

def pair_terms(rvec, source_feat, layer_one, layer_two, layer_three):
    squared = lax.optimization_barrier(jnp.sum(rvec * rvec, axis=0))
    envelope = jnp.square(jnp.maximum(1.0 - squared / cutoff_square, 0.0))
    count_basis = layer_one.shape[1]
    centers = jnp.arange(count_basis).astype(jnp.float32) * (cutoff_square / (count_basis - 1))
    basis = jnp.exp(-jnp.square(squared[None, :] - centers[:, None]) / basis_width) * envelope[None, :]
    hidden_one = jax.nn.silu(jnp.dot(layer_one, basis, precision=lax.Precision.HIGHEST))
    hidden_two = jax.nn.silu(jnp.dot(layer_two, hidden_one, precision=lax.Precision.HIGHEST))
    radial = jnp.dot(layer_three, hidden_two, precision=lax.Precision.HIGHEST)
    channels = source_feat.shape[0]
    weighted = radial.reshape(3, channels, -1) * source_feat[None] * message_scale
    unit = rvec * 0.5
    ux, uy, uz = (unit[0], unit[1], unit[2])
    second = jnp.stack([root_three * ux * uy, root_three * uy * uz, 0.5 * (2.0 * uz * uz - ux * ux - uy * uy), root_three * ux * uz, 0.5 * root_three * (ux * ux - uy * uy)], 0)
    return jnp.concatenate([weighted[0][None], weighted[1][None] * unit[:, None], weighted[2][None] * second[:, None]], 0)

def atom_energy(moments, kinds, species_shift, inv_matrix, head_vector):
    invariants = jnp.concatenate([moments[0], lax.optimization_barrier(jnp.sum(moments[1:4] ** 2, axis=0)), lax.optimization_barrier(jnp.sum(moments[4:9] ** 2, axis=0))], 0)
    mixed = jnp.dot(inv_matrix, invariants, precision=lax.Precision.HIGHEST)
    count_kinds = species_shift.shape[0]
    onehot = (kinds[None, :] == jnp.arange(count_kinds).astype(jnp.int32)[:, None]).astype(species_shift.dtype)
    return jnp.dot(head_vector, jax.nn.silu(mixed), precision=lax.Precision.HIGHEST) + jnp.dot(species_shift, onehot, precision=lax.Precision.HIGHEST)

def reference(positions, features, species, species_shift, send_index, pair_target, pair_source, block_count, radial_first, radial_second, radial_third, invariant_mix, energy_head):
    layers = (radial_first.astype(jnp.float32).T, radial_second.astype(jnp.float32).T, radial_third.astype(jnp.float32).T)
    inv_matrix = invariant_mix.astype(jnp.float32).T
    head_vector = energy_head.astype(jnp.float32)
    shift_table = species_shift.astype(jnp.float32)
    slab_side = cell_side * K
    slabs = N_GX * N_GY * N_GZ
    chosen = send_index[:, :, :, None, :]
    border_feat = jnp.take_along_axis(features, jnp.broadcast_to(chosen, (N_GX, N_GY, N_GZ, CH, G)), axis=4)
    ghost_feat = []
    for slot in range(27):
        offs = (1 - slot // 9, 1 - slot // 3 % 3, 1 - slot % 3)
        ghost_feat.append(jnp.roll(border_feat, offs, axis=(0, 1, 2)))
    table_feat = jnp.concatenate([features] + ghost_feat, axis=4).reshape(slabs, CH, A + 27 * G)
    kinds_all = species.reshape(slabs, A)
    targets_all = pair_target.reshape(slabs, NB, PB)
    sources_all = pair_source.reshape(slabs, NB, PB)
    counts_all = block_count.reshape(slabs)

    def energies_of(pos_full):
        border_pos = jnp.take_along_axis(pos_full, jnp.broadcast_to(chosen, (N_GX, N_GY, N_GZ, 3, G)), axis=4)
        ghost_pos = []
        for slot in range(27):
            offs = (1 - slot // 9, 1 - slot // 3 % 3, 1 - slot % 3)
            moved = jnp.array([-offs[0], -offs[1], -offs[2]], dtype=pos_full.dtype) * slab_side
            ghost_pos.append(jnp.roll(border_pos, offs, axis=(0, 1, 2)) + moved[:, None])
        table_pos = jnp.concatenate([pos_full] + ghost_pos, axis=4).reshape(slabs, 3, A + 27 * G)
        own_pos = pos_full.reshape(slabs, 3, A)

        def one_slab(inputs):
            tpos, tfeat, opos, kinds, targets, sources, count = inputs

            def block(moments, block_index):
                target = targets[block_index]
                source = sources[block_index]
                rvec = jnp.take(tpos, source, axis=1) - jnp.take(opos, target, axis=1)
                source_feat = jnp.take(tfeat, source, axis=1).astype(pos_full.dtype)
                terms = pair_terms(rvec, source_feat, *layers) * (block_index < count).astype(pos_full.dtype)
                return (moments.at[:, :, target].add(terms), None)
            start = jnp.zeros((9, CH, A), pos_full.dtype)
            moments, _ = lax.scan(jax.checkpoint(block), start, jnp.arange(NB).astype(jnp.int32))
            return atom_energy(moments, kinds, shift_table, inv_matrix, head_vector)
        result = lax.map(jax.checkpoint(one_slab), (table_pos, table_feat, own_pos, kinds_all, targets_all, sources_all, counts_all))
        return result.reshape(N_GX, N_GY, N_GZ, A)
    pos_full = positions.astype(jnp.float32)
    energies, pull = jax.vjp(energies_of, pos_full)
    grad_pos, = pull(jnp.ones_like(energies))
    return (energies, -grad_pos)
```

```python
import functools

import jax
import jax.numpy as jnp
import numpy as np
from jax import lax
from jax.experimental import pallas as pl
from jax.experimental.pallas import tpu as pltpu
from jax.sharding import PartitionSpec as P

A = 432
AP = 512
G = 304
CH = 128
NB = 10
PB = 128
BL = 256
STEPS = NB * PB // BL
RH = 64
NRB = 8
SPECIES = 10
GT = 1280
SENT = 1088
CELL = 2.5
SIDE = 15.0
CUT = 25.0
MID = 152.0
SCALE = 0.15
ROOT3 = 1.7320508075688772

F32 = jnp.float32
BF16 = jnp.bfloat16
MESH = pl.DeviceIdType.MESH
NN = (((1,), (0,)), ((), ()))
NT = (((1,), (1,)), ((), ()))


def offset_of(slot):
    return (slot // 9 - 1, slot // 3 % 3 - 1, slot % 3 - 1)


def places():
    by_kind = {1: [], 2: [], 3: []}
    for slot in range(27):
        if slot != 13:
            by_kind[sum(abs(c) for c in offset_of(slot))].append(slot)
    out = []
    for i, slot in enumerate(by_kind[1]):
        out.append((slot, 96, 96 * i, 128 * i))
    for i, slot in enumerate(by_kind[2]):
        out.append((slot, 32, 576 + 32 * i, 768 + 32 * i))
    for i, slot in enumerate(by_kind[3]):
        out.append((slot, 16, 960 + 16 * i, 1152 + 16 * i))
    return out


PLACES = places()


def dot(a, b, dims=NN):
    return lax.dot_general(a, b, dims, preferred_element_type=F32)


def iota(shape, dim):
    return lax.broadcasted_iota(jnp.int32, shape, dim)


def high_low(x):
    high = x.astype(BF16).astype(F32)
    return high, x - high


def neighbour(slot, sign):
    where = []
    for axis, size, step in zip(("gx", "gy", "gz"), (4, 4, 16), offset_of(slot)):
        me = lax.axis_index(axis)
        where.append(lax.rem(me + (size + sign * step), size) if step else me)
    return tuple(where)


def enter():
    barrier = pltpu.get_barrier_semaphore()
    for slot, *_ in PLACES:
        pl.semaphore_signal(
            barrier, inc=1, device_id=neighbour(slot, 1), device_id_type=MESH
        )
    return barrier


def choose(pos_ref, feat_ref, list_ref, pick_ref, send_ref):
    pos = pos_ref[...].astype(F32)
    entry = (iota((A, G), 0) == list_ref[...]).astype(BF16)
    ids = iota((8, G), 1).astype(F32)
    coded = jnp.where(ids < MID, ids - MID, ids - (MID - 1.0))
    code = dot(coded.astype(BF16), entry, NT)
    member = (code[0:1] != 0.0).astype(F32)
    slots = iota((32, A), 0)
    ix = (slots >= 9).astype(jnp.int32) + (slots >= 18).astype(jnp.int32)
    rest = slots - 9 * ix
    iy = (rest >= 3).astype(jnp.int32) + (rest >= 6).astype(jnp.int32)
    iz = rest - 3 * iy
    strict = member
    closed = member
    for axis, index in enumerate((ix, iy, iz)):
        x = pos[axis : axis + 1]
        one = jnp.ones((1, A), F32)
        strict = strict * jnp.where(
            index == 0,
            (x > SIDE - CELL).astype(F32),
            jnp.where(index == 2, (x < CELL).astype(F32), one),
        )
        closed = closed * jnp.where(
            index == 0,
            (x >= SIDE - CELL).astype(F32),
            jnp.where(index == 2, (x <= CELL).astype(F32), one),
        )
    both = jnp.concatenate([strict, closed - strict], 0)
    upper = (iota((A, A), 0) <= iota((A, A), 1)).astype(BF16)
    count = dot(both.astype(BF16), upper)
    total = count[:32, A - 1 : A]
    rank = jnp.where(
        strict > 0.0,
        count[:32] - 1.0,
        jnp.where(closed > 0.0, total + count[32:] - 1.0, -1.0),
    )
    for slot, rows, _, lane in PLACES:
        tall = 128 if rows == 96 else rows
        step = iota((tall, A), 0)
        step = jnp.where(step < rows - 4, step, -2).astype(F32)
        pick_ref[lane : lane + tall, :] = (step == rank[slot : slot + 1]).astype(BF16)
    meta = jnp.concatenate([jnp.zeros((4, A), F32), pos, code[0:1]], 0).astype(BF16)
    for slot, rows, row, lane in PLACES:
        if rows == 96:
            block = dot(pick_ref[lane : lane + 128, :], feat_ref[...], NT)
            told = dot(meta, pick_ref[lane : lane + 128, :], NT)
            out = jnp.concatenate([block[:88], block[88:96] + told], 0)
            send_ref[row : row + 96, :] = out.astype(BF16)
    for group in range(4):
        start = 768 + 128 * group
        rows = 32 if group < 3 else 16
        block = dot(pick_ref[start : start + 128, :], feat_ref[...], NT)
        told = dot(meta, pick_ref[start : start + 128, :], NT)
        pieces = []
        for i in range(128 // rows):
            pieces.append(block[rows * i : rows * i + rows - 8])
            pieces.append(block[rows * i + rows - 8 : rows * (i + 1)] + told)
        row = 576 + 128 * group
        send_ref[row : row + 128, :] = jnp.concatenate(pieces, 0).astype(BF16)


def exchange_kernel(
    pos_ref, feat_ref, list_ref, pick_ref, got_ref, send_ref, send_sem, recv_sem
):
    barrier = enter()
    choose(pos_ref, feat_ref, list_ref, pick_ref, send_ref)
    pl.semaphore_wait(barrier, 26)
    copies = []
    for i, (slot, rows, row, _) in enumerate(PLACES):
        copies.append(
            pltpu.make_async_remote_copy(
                src_ref=send_ref.at[row : row + rows, :],
                dst_ref=got_ref.at[row : row + rows, :],
                send_sem=send_sem.at[i],
                recv_sem=recv_sem.at[i],
                device_id=neighbour(slot, -1),
                device_id_type=MESH,
            )
        )
        copies[-1].start()
    for copy in copies:
        copy.wait()


def group_lanes(tiles, width):
    lane = iota(tiles[0].shape, 1)
    out = tiles[0]
    for i in range(1, len(tiles)):
        out = jnp.where(lane >= width * i, tiles[i], out)
    return out


def ghost_table(got_ref, table_ref, key_ref):
    tiles = [[] for _ in range(10)]
    for place in PLACES:
        tiles[place[3] // 128].append(place)
    for t, members in enumerate(tiles):
        width = 128 // len(members)
        row, rows = members[0][2], members[0][1]
        if rows == 96:
            feats = jnp.concatenate(
                [got_ref[row : row + 96, :].astype(F32), jnp.zeros((32, CH), F32)], 0
            )
        else:
            feats = got_ref[row : row + 128, :].astype(F32)
        table_ref[0:CH, 128 * t : 128 * (t + 1)] = feats.T.astype(BF16)
        told, offs = [], []
        for slot, rows, row, _ in members:
            told.append(got_ref[row + rows - 16 : row + rows, :].astype(F32)[8:16])
        told = group_lanes(told, width)
        sub = iota((8, 128), 0)
        for slot, *_ in members:
            o = offset_of(slot)
            offs.append(
                jnp.where(
                    sub == 0,
                    float(o[0]),
                    jnp.where(sub == 1, float(o[1]), jnp.where(sub == 2, float(o[2]), 0.0)),
                )
            )
        offs = group_lanes(offs, width)
        base = group_lanes(
            [jnp.full((8, 128), float(A + G * slot), F32) for slot, *_ in members], width
        )
        table_ref[CH : CH + 16, 128 * t : 128 * (t + 1)] = jnp.concatenate(
            [told, offs], 0
        ).astype(BF16)
        code = told[7:8]
        index = jnp.where(code < 0.0, code + MID, code + (MID - 1.0)) + base[0:1]
        key = jnp.where(code == 0.0, -5.0, index)
        column = jnp.broadcast_to(key, (128, 128)).T.astype(jnp.int32)
        key_ref[128 * t : 128 * (t + 1), :] = jnp.concatenate([column, column], 1)


def silu_parts(z):
    s = 0.5 * jnp.tanh(0.5 * z) + 0.5
    h = z * s
    return h, s + h * (1.0 - s)


def stack_high_low(x):
    return jnp.concatenate(high_low(x), 0).astype(BF16)


def main_kernel(
    count_ref,
    shift_ref,
    pos_ref,
    feat_ref,
    got_ref,
    species_ref,
    target_ref,
    source_ref,
    first_ref,
    second_ref,
    third_ref,
    mix_ref,
    head_ref,
    energy_ref,
    own_ref,
    ghost_ref,
    own_table,
    table,
    keys,
    from_own,
    from_ghost,
    to_own,
    radial_ref,
    slope_ref,
    geom_ref,
    terms_ref,
    moments,
    grads,
    back_ref,
):
    count = count_ref[0]
    ghost_table(got_ref, table, keys)
    own_table[...] = jnp.zeros_like(own_table)
    own_table[0:CH, 0:A] = feat_ref[...]
    pos = jnp.concatenate([pos_ref[...].astype(F32), jnp.zeros((13, A), F32)], 0)
    own_table[CH : CH + 16, 0:A] = pos.astype(BF16)
    first = first_ref[...].astype(F32).T
    first = jnp.concatenate([first, first], 1).astype(BF16)
    second = second_ref[...].astype(F32).T
    second = jnp.concatenate([second, second], 1).astype(BF16)
    third = third_ref[...].astype(F32).T
    third = jnp.concatenate([third, third], 1).astype(BF16)
    moments[...] = jnp.zeros_like(moments)

    def pair_rows(ref, b):
        return jnp.concatenate([ref[pl.ds(2 * b, 1), :], ref[pl.ds(2 * b + 1, 1), :]], 1)

    def forward(b, carry):
        source = pair_rows(source_ref, b)
        target = pair_rows(target_ref, b)
        live = 2 * b + (iota((1, BL), 1) >= PB).astype(jnp.int32) < count
        target = jnp.where(live, target, -1)
        atoms = iota((AP, BL), 0)
        pick_own = (atoms == source).astype(BF16)
        pick_ghost = (keys[...] == source).astype(BF16)
        pick_target = (atoms == target).astype(BF16)
        from_own[b] = pick_own
        from_ghost[b] = pick_ghost
        to_own[b, 0:AP, :] = pick_target
        to_own[b, AP : 2 * AP, :] = pick_target
        near = dot(own_table[...], pick_own)
        far = dot(table[...], pick_ghost)
        feats = (near[:CH] + far[:CH]) * SCALE
        here = dot(own_table[CH : CH + 16, :], pick_target)
        r = (
            (near[CH : CH + 3] + far[CH + 4 : CH + 7])
            + SIDE * far[CH + 8 : CH + 11]
            - here[0:3]
        )
        q = r[0:1] * r[0:1] + r[1:2] * r[1:2] + r[2:3] * r[2:3]
        keep = jnp.maximum(1.0 - q / CUT, 0.0)
        envelope = keep * keep
        d_envelope = keep * (-2.0 / CUT)
        centers = iota((NRB, BL), 0).astype(F32) * (CUT / (NRB - 1))
        away = q - centers
        bump = jnp.exp(-(away * away) / CUT)
        basis = bump * envelope
        d_basis = bump * (d_envelope - (2.0 / CUT) * away * envelope)
        z = dot(first, jnp.concatenate([stack_high_low(basis), stack_high_low(d_basis)], 1))
        h, slope = silu_parts(z[:, :BL])
        d = slope * z[:, BL:]
        z = dot(second, jnp.concatenate([stack_high_low(h), stack_high_low(d)], 1))
        h, slope = silu_parts(z[:, :BL])
        d = slope * z[:, BL:]
        z = dot(third, jnp.concatenate([stack_high_low(h), stack_high_low(d)], 1))
        ux, uy, uz = 0.5 * r[0:1], 0.5 * r[1:2], 0.5 * r[2:3]
        harmonics = [
            [None],
            [ux, uy, uz],
            [
                ROOT3 * ux * uy,
                ROOT3 * uy * uz,
                0.5 * (2.0 * uz * uz - ux * ux - uy * uy),
                ROOT3 * ux * uz,
                0.5 * ROOT3 * (ux * ux - uy * uy),
            ],
        ]
        geom_ref[b] = jnp.concatenate([r, jnp.zeros((5, BL), F32)], 0)
        row = 0
        for order in range(3):
            weighted = z[CH * order : CH * (order + 1), :BL] * feats
            radial_ref[b, CH * order : CH * (order + 1), :] = weighted
            slope_ref[b, CH * order : CH * (order + 1), :] = (
                z[CH * order : CH * (order + 1), BL:] * feats
            )
            for harmonic in harmonics[order]:
                term = weighted if harmonic is None else weighted * harmonic
                high, low = high_low(term)
                terms_ref[row : row + CH, 0:BL] = high.astype(BF16)
                terms_ref[row : row + CH, BL : 2 * BL] = low.astype(BF16)
                row += CH
        twice = jnp.concatenate([pick_target, pick_target], 1)
        moments[...] += dot(terms_ref[...], twice, NT)
        return carry

    lax.fori_loop(0, STEPS, forward, 0)

    def moment(i):
        return moments[CH * i : CH * (i + 1), :]

    squares = []
    for low, high in ((1, 4), (4, 9)):
        total = moment(low) * moment(low)
        for i in range(low + 1, high):
            total = total + moment(i) * moment(i)
        squares.append(total)
    invariants = jnp.concatenate([moment(0)] + squares, 0)
    mix = mix_ref[...]
    mix_t = mix.astype(F32).T.astype(BF16)
    high, low = high_low(invariants)
    mixed = dot(mix_t, high.astype(BF16)) + dot(mix_t, low.astype(BF16))
    head = jnp.broadcast_to(head_ref[...].astype(F32), (128, 128)).T
    head = jnp.concatenate([head] * 4, 1)
    h, slope = silu_parts(mixed)
    energy = jnp.sum(head * h, axis=0, keepdims=True)[:, :A]
    kinds = species_ref[...]
    for k in range(SPECIES):
        energy = energy + jnp.where(kinds == k, shift_ref[k], 0.0)
    energy_ref[...] = energy
    d_mixed = stack_high_low(head * slope)
    d_inv = dot(jnp.concatenate([mix, mix], 1), d_mixed)
    for i in range(9):
        order = 0 if i == 0 else (1 if i < 4 else 2)
        grad = d_inv[CH * order : CH * (order + 1)]
        if order:
            grad = 2.0 * moment(i) * grad
        high, low = high_low(grad)
        grads[CH * i : CH * (i + 1), 0:AP] = high.astype(BF16)
        grads[CH * i : CH * (i + 1), AP : 2 * AP] = low.astype(BF16)
    own_ref[...] = jnp.zeros_like(own_ref)
    ghost_ref[...] = jnp.zeros_like(ghost_ref)

    def backward(b, carry):
        back_ref[...] = dot(grads[...], to_own[b])
        r = geom_ref[b]
        along, across = [], []
        for i in range(9):
            order = 0 if i == 0 else (1 if i < 4 else 2)
            grad = back_ref[CH * i : CH * (i + 1), :]
            if order:
                along.append(
                    jnp.sum(
                        radial_ref[b, CH * order : CH * (order + 1), :] * grad,
                        axis=0,
                        keepdims=True,
                    )
                )
            across.append(
                jnp.sum(
                    slope_ref[b, CH * order : CH * (order + 1), :] * grad,
                    axis=0,
                    keepdims=True,
                )
            )
        ux, uy, uz = 0.5 * r[0:1], 0.5 * r[1:2], 0.5 * r[2:3]
        ax, ay, az, b0, b1, b2, b3, b4 = along
        dq = (
            across[0]
            + ux * across[1]
            + uy * across[2]
            + uz * across[3]
            + (ROOT3 * ux * uy) * across[4]
            + (ROOT3 * uy * uz) * across[5]
            + (0.5 * (2.0 * uz * uz - ux * ux - uy * uy)) * across[6]
            + (ROOT3 * ux * uz) * across[7]
            + (0.5 * ROOT3 * (ux * ux - uy * uy)) * across[8]
        )
        gx = ax + ROOT3 * (uy * b0 + uz * b3 + ux * b4) - ux * b2
        gy = ay + ROOT3 * (ux * b0 + uz * b1 - uy * b4) - uy * b2
        gz = az + ROOT3 * (uy * b1 + ux * b3) + 2.0 * uz * b2
        px = 0.5 * gx + 2.0 * dq * r[0:1]
        py = 0.5 * gy + 2.0 * dq * r[1:2]
        pz = 0.5 * gz + 2.0 * dq * r[2:3]
        pull = jnp.concatenate([px, py, pz, jnp.zeros((5, BL), F32)], 0)
        pull = stack_high_low(pull)
        own = dot(pull, to_own[b, 0:AP, :] - from_own[b], NT)
        ghost = dot(pull, from_ghost[b], NT)
        own_ref[...] += own[:8] + own[8:]
        ghost_ref[...] -= ghost[:8] + ghost[8:]
        return carry

    lax.fori_loop(0, STEPS, backward, 0)


def return_kernel(ghost_ref, own_ref, pick_ref, force_ref, got_ref, send_sem, recv_sem):
    barrier = enter()
    pl.semaphore_wait(barrier, 26)
    copies = []
    for i, (slot, rows, _, lane) in enumerate(PLACES):
        start = lane // 128 * 128
        copies.append(
            pltpu.make_async_remote_copy(
                src_ref=ghost_ref.at[:, start : start + 128],
                dst_ref=got_ref.at[i],
                send_sem=send_sem.at[i],
                recv_sem=recv_sem.at[i],
                device_id=neighbour(slot, 1),
                device_id_type=MESH,
            )
        )
        copies[-1].start()
    for copy in copies:
        copy.wait()
    tiles = [[] for _ in range(10)]
    for i, place in enumerate(PLACES):
        tiles[place[3] // 128].append(got_ref[i])
    tiles = [group_lanes(members, 128 // len(members)) for members in tiles]
    sums = dot(stack_high_low(jnp.concatenate(tiles, 1)), pick_ref[...])
    total = own_ref[:, :A] + sums[:8] + sums[8:]
    force_ref[...] = total[:3]


def vmem():
    return pl.BlockSpec(memory_space=pltpu.VMEM)


def smem():
    return pl.BlockSpec(memory_space=pltpu.SMEM)


def shape(dims, kind=F32):
    return jax.ShapeDtypeStruct(dims, kind)


def shards(
    positions,
    features,
    species,
    species_shift,
    send_index,
    pair_target,
    pair_source,
    block_count,
    radial_first,
    radial_second,
    radial_third,
    invariant_mix,
    energy_head,
):
    pos = positions.reshape(3, A)
    feat = features.reshape(CH, A)
    pick, got = pl.pallas_call(
        exchange_kernel,
        out_shape=(shape((GT, A), BF16), shape((SENT, CH), BF16)),
        in_specs=[vmem()] * 3,
        out_specs=(vmem(), vmem()),
        scratch_shapes=[
            pltpu.VMEM((SENT, CH), BF16),
            pltpu.SemaphoreType.DMA((26,)),
            pltpu.SemaphoreType.DMA((26,)),
        ],
        compiler_params=pltpu.CompilerParams(
            collective_id=0, has_side_effects=True, vmem_limit_bytes=24 * 2**20
        ),
        name="exchange",
    )(pos, feat, send_index.reshape(1, G))
    energies, own, ghost = pl.pallas_call(
        main_kernel,
        out_shape=(shape((1, A)), shape((8, AP)), shape((8, GT))),
        in_specs=[smem()] * 2 + [vmem()] * 11,
        out_specs=(vmem(), vmem(), vmem()),
        scratch_shapes=[
            pltpu.VMEM((CH + 16, AP), BF16),
            pltpu.VMEM((CH + 16, GT), BF16),
            pltpu.VMEM((GT, BL), jnp.int32),
            pltpu.VMEM((STEPS, AP, BL), BF16),
            pltpu.VMEM((STEPS, GT, BL), BF16),
            pltpu.VMEM((STEPS, 2 * AP, BL), BF16),
            pltpu.VMEM((STEPS, 3 * CH, BL), F32),
            pltpu.VMEM((STEPS, 3 * CH, BL), F32),
            pltpu.VMEM((STEPS, 8, BL), F32),
            pltpu.VMEM((9 * CH, 2 * BL), BF16),
            pltpu.VMEM((9 * CH, AP), F32),
            pltpu.VMEM((9 * CH, 2 * AP), BF16),
            pltpu.VMEM((9 * CH, BL), F32),
        ],
        compiler_params=pltpu.CompilerParams(vmem_limit_bytes=48 * 2**20),
        name="interact",
    )(
        block_count.reshape(1),
        species_shift,
        pos,
        feat,
        got,
        species.reshape(1, A),
        pair_target.reshape(NB, PB),
        pair_source.reshape(NB, PB),
        radial_first,
        radial_second,
        radial_third,
        invariant_mix,
        energy_head.reshape(1, CH),
    )
    forces = pl.pallas_call(
        return_kernel,
        out_shape=shape((3, A)),
        in_specs=[vmem()] * 3,
        out_specs=vmem(),
        scratch_shapes=[
            pltpu.VMEM((26, 8, 128), F32),
            pltpu.SemaphoreType.DMA((26,)),
            pltpu.SemaphoreType.DMA((26,)),
        ],
        compiler_params=pltpu.CompilerParams(
            collective_id=1, has_side_effects=True, vmem_limit_bytes=24 * 2**20
        ),
        name="give_back",
    )(ghost, own, pick)
    return (energies.reshape(1, 1, 1, A), forces.reshape(1, 1, 1, 3, A))


def solution(mesh):
    split = ("gx", "gy", "gz")
    return jax.shard_map(
        shards,
        mesh=mesh,
        in_specs=(
            P(*split, None, None),
            P(*split, None, None),
            P(*split, None),
            P(),
            P(*split, None),
            P(*split, None, None),
            P(*split, None, None),
            P(*split),
            P(),
            P(),
            P(),
            P(),
            P(),
        ),
        out_specs=(P(*split, None), P(*split, None, None)),
        check_vma=False,
    )
```

```python
import functools

import jax
import jax.numpy as jnp
import numpy as np
from jax import lax
from jax.experimental import pallas as pl
from jax.experimental.pallas import tpu as pltpu
from jax.sharding import PartitionSpec as P

A = 432
AP = 512
G = 304
CH = 128
NB = 10
PB = 128
BL = 256
STEPS = NB * PB // BL
NP = NB * PB
RH = 64
NRB = 8
SPECIES = 10
GT = 1280
SENT = 1088
CELL = 2.5
SIDE = 15.0
CUT = 25.0
MID = 152.0
SCALE = 0.15
ROOT3 = 1.7320508075688772

F32 = jnp.float32
BF16 = jnp.bfloat16
MESH = pl.DeviceIdType.MESH
KEY = jnp.int32
NN = (((1,), (0,)), ((), ()))
NT = (((1,), (1,)), ((), ()))


def offset_of(slot):
    return (slot // 9 - 1, slot // 3 % 3 - 1, slot % 3 - 1)


def places():
    by_kind = {1: [], 2: [], 3: []}
    for slot in range(27):
        if slot != 13:
            by_kind[sum(abs(c) for c in offset_of(slot))].append(slot)
    out = []
    for i, slot in enumerate(by_kind[1]):
        out.append((slot, 96, 96 * i, 128 * i))
    for i, slot in enumerate(by_kind[2]):
        out.append((slot, 32, 576 + 32 * i, 768 + 32 * i))
    for i, slot in enumerate(by_kind[3]):
        out.append((slot, 16, 960 + 16 * i, 1152 + 16 * i))
    return out


PLACES = places()


def dot(a, b, dims=NN):
    return lax.dot_general(a, b, dims, preferred_element_type=F32)


def iota(shape, dim):
    return lax.broadcasted_iota(jnp.int32, shape, dim)


def high_low(x):
    high = x.astype(BF16).astype(F32)
    return high, x - high


def neighbour(slot, sign):
    where = []
    for axis, size, step in zip(("gx", "gy", "gz"), (4, 4, 16), offset_of(slot)):
        me = lax.axis_index(axis)
        where.append(lax.rem(me + (size + sign * step), size) if step else me)
    return tuple(where)


def enter():
    barrier = pltpu.get_barrier_semaphore()
    for slot, *_ in PLACES:
        pl.semaphore_signal(
            barrier, inc=1, device_id=neighbour(slot, 1), device_id_type=MESH
        )
    return barrier


def choose(pos_ref, feat_ref, list_ref, pick_ref, send_ref):
    pos = pos_ref[...].astype(F32)
    entry = (iota((A, G), 0) == list_ref[...]).astype(BF16)
    ids = iota((8, G), 1).astype(F32)
    coded = jnp.where(ids < MID, ids - MID, ids - (MID - 1.0))
    code = dot(coded.astype(BF16), entry, NT)
    member = (code[0:1] != 0.0).astype(F32)
    slots = iota((32, A), 0)
    ix = (slots >= 9).astype(jnp.int32) + (slots >= 18).astype(jnp.int32)
    rest = slots - 9 * ix
    iy = (rest >= 3).astype(jnp.int32) + (rest >= 6).astype(jnp.int32)
    iz = rest - 3 * iy
    strict = member
    closed = member
    for axis, index in enumerate((ix, iy, iz)):
        x = pos[axis : axis + 1]
        one = jnp.ones((1, A), F32)
        strict = strict * jnp.where(
            index == 0,
            (x > SIDE - CELL).astype(F32),
            jnp.where(index == 2, (x < CELL).astype(F32), one),
        )
        closed = closed * jnp.where(
            index == 0,
            (x >= SIDE - CELL).astype(F32),
            jnp.where(index == 2, (x <= CELL).astype(F32), one),
        )
    both = jnp.concatenate([strict, closed - strict], 0)
    upper = (iota((A, A), 0) <= iota((A, A), 1)).astype(BF16)
    count = dot(both.astype(BF16), upper)
    total = count[:32, A - 1 : A]
    rank = jnp.where(
        strict > 0.0,
        count[:32] - 1.0,
        jnp.where(closed > 0.0, total + count[32:] - 1.0, -1.0),
    )
    for slot, rows, _, lane in PLACES:
        tall = 128 if rows == 96 else rows
        step = iota((tall, A), 0)
        step = jnp.where(step < rows - 4, step, -2).astype(F32)
        pick_ref[lane : lane + tall, :] = (step == rank[slot : slot + 1]).astype(BF16)
    meta = jnp.concatenate([jnp.zeros((4, A), F32), pos, code[0:1]], 0).astype(BF16)
    feat = feat_ref[...]
    for slot, rows, row, lane in PLACES:
        if rows == 96:
            block = dot(pick_ref[lane : lane + 96, :], feat)
            told = dot(meta, pick_ref[lane : lane + 128, :], NT)
            out = jnp.concatenate([block[:88], block[88:96] + told], 0)
            send_ref[row : row + 96, :] = out.astype(BF16)
    for group in range(4):
        start = 768 + 128 * group
        rows = 32 if group < 3 else 16
        block = dot(pick_ref[start : start + 128, :], feat)
        told = dot(meta, pick_ref[start : start + 128, :], NT)
        pieces = []
        for i in range(128 // rows):
            pieces.append(block[rows * i : rows * i + rows - 8])
            pieces.append(block[rows * i + rows - 8 : rows * (i + 1)] + told)
        row = 576 + 128 * group
        send_ref[row : row + 128, :] = jnp.concatenate(pieces, 0).astype(BF16)


def group_lanes(tiles, width):
    lane = iota(tiles[0].shape, 1)
    out = tiles[0]
    for i in range(1, len(tiles)):
        out = jnp.where(lane >= width * i, tiles[i], out)
    return out


def ghost_table(got_ref, table_ref, key_ref):
    tiles = [[] for _ in range(10)]
    for place in PLACES:
        tiles[place[3] // 128].append(place)
    for t, members in enumerate(tiles):
        width = 128 // len(members)
        row, rows = members[0][2], members[0][1]
        if rows == 96:
            feats = jnp.concatenate(
                [got_ref[row : row + 96, :].astype(F32), jnp.zeros((32, CH), F32)], 0
            )
        else:
            feats = got_ref[row : row + 128, :].astype(F32)
        table_ref[0:CH, 128 * t : 128 * (t + 1)] = feats.T.astype(BF16)
        told, offs = [], []
        for slot, rows, row, _ in members:
            told.append(got_ref[row + rows - 16 : row + rows, :].astype(F32)[8:16])
        told = group_lanes(told, width)
        sub = iota((8, 128), 0)
        for slot, *_ in members:
            o = offset_of(slot)
            offs.append(
                jnp.where(
                    sub == 0,
                    float(o[0]),
                    jnp.where(sub == 1, float(o[1]), jnp.where(sub == 2, float(o[2]), 0.0)),
                )
            )
        offs = group_lanes(offs, width)
        base = group_lanes(
            [jnp.full((8, 128), float(A + G * slot), F32) for slot, *_ in members], width
        )
        table_ref[CH : CH + 16, 128 * t : 128 * (t + 1)] = jnp.concatenate(
            [told, offs], 0
        ).astype(BF16)
        code = told[7:8]
        index = jnp.where(code < 0.0, code + MID, code + (MID - 1.0)) + base[0:1]
        key = jnp.where(code == 0.0, -5.0, index)
        column = jnp.broadcast_to(key, (128, 128)).T.astype(KEY)
        key_ref[128 * t : 128 * (t + 1), :] = jnp.concatenate([column, column], 1)


def silu_parts(z):
    s = 0.5 * jnp.tanh(0.5 * z) + 0.5
    h = z * s
    return h, s + h * (1.0 - s)


def stack_high_low(x):
    return jnp.concatenate(high_low(x), 0).astype(BF16)


def span(b):
    return pl.ds(pl.multiple_of(b * BL, BL), BL)


def pair_rows(ref, b):
    return jnp.concatenate([ref[2 * b], ref[2 * b + 1]], 1)


def twice_across(ref):
    x = ref[...].astype(F32).T
    return jnp.concatenate([x, x], 1).astype(BF16)


def prepare(r):
    r.own_table[...] = jnp.zeros_like(r.own_table)
    feat = r.feat[...].astype(F32).T
    r.own_table[0:CH, 0:A] = feat.astype(BF16)
    pos = jnp.concatenate([r.pos[...].astype(F32), jnp.zeros((13, A), F32)], 0)
    r.own_table[CH : CH + 16, 0:A] = pos.astype(BF16)
    count = r.count[0, 0, 0]

    def near_step(b, carry):
        source = pair_rows(r.source, b)
        target = pair_rows(r.target, b)
        live = 2 * b + (iota((1, BL), 1) >= PB).astype(jnp.int32) < count
        target = jnp.where(live, target, -1)
        atoms = iota((AP, BL), 0)
        pick_own = (atoms == source).astype(BF16)
        pick_target = (atoms == target).astype(BF16)
        r.from_own[b] = pick_own
        r.to_own[b, 0:AP, :] = pick_target
        r.to_own[b, AP : 2 * AP, :] = pick_target
        near = dot(r.own_table[...], pick_own)
        here = dot(r.own_table[CH : CH + 16, :], pick_target)
        r.near[:, span(b)] = jnp.concatenate([near[:CH], near[CH : CH + 8] - here[:8]], 0)
        return carry

    lax.fori_loop(0, STEPS, near_step, 0)


def gather(r):
    def far_step(b, carry):
        source = pair_rows(r.source, b)
        pick_ghost = (r.keys[...] == source.astype(KEY)).astype(BF16)
        r.from_ghost[b] = pick_ghost
        far = dot(r.table[...], pick_ghost)
        near = r.near[:, span(b)]
        r.feats[:, span(b)] = (near[:CH] + far[:CH]) * SCALE
        r.geom[0:3, span(b)] = (
            near[CH : CH + 3] + far[CH + 4 : CH + 7] + SIDE * far[CH + 8 : CH + 11]
        )
        return carry

    lax.fori_loop(0, STEPS, far_step, 0)


def harmonics_of(x, y, z):
    return [
        ROOT3 * x * y,
        ROOT3 * y * z,
        0.5 * (2.0 * z * z - x * x - y * y),
        ROOT3 * x * z,
        0.5 * ROOT3 * (x * x - y * y),
    ]


def radial(r):
    v = r.geom[0:3, :]
    q = v[0:1] * v[0:1] + v[1:2] * v[1:2] + v[2:3] * v[2:3]
    keep = jnp.maximum(1.0 - q / CUT, 0.0)
    envelope = keep * keep
    d_envelope = keep * (-2.0 / CUT)
    centers = iota((NRB, NP), 0).astype(F32) * (CUT / (NRB - 1))
    away = q - centers
    bump = jnp.exp(-(away * away) / CUT)
    basis = bump * envelope
    d_basis = bump * (d_envelope - (2.0 / CUT) * away * envelope)
    first = twice_across(r.first)
    z = dot(first, jnp.concatenate([stack_high_low(basis), stack_high_low(d_basis)], 1))
    h, slope = silu_parts(z[:, :NP])
    d = slope * z[:, NP:]
    second = twice_across(r.second)
    z = dot(second, jnp.concatenate([stack_high_low(h), stack_high_low(d)], 1))
    h, slope = silu_parts(z[:, :NP])
    d = slope * z[:, NP:]
    r.hidden[0] = stack_high_low(h)
    r.hidden[1] = stack_high_low(d)


def scatter(r):
    third = twice_across(r.third)
    r.moments[...] = jnp.zeros_like(r.moments)

    def step(b, carry):
        feats = r.feats[:, span(b)]
        v = r.geom[0:3, span(b)]
        z = dot(third, r.hidden[0, :, span(b)])
        d = dot(third, r.hidden[1, :, span(b)])
        ux, uy, uz = 0.5 * v[0:1], 0.5 * v[1:2], 0.5 * v[2:3]
        harmonics = [[None], [ux, uy, uz], harmonics_of(ux, uy, uz)]
        row = 0
        for order in range(3):
            part = slice(CH * order, CH * (order + 1))
            weighted = z[part] * feats
            r.radial[b, part, :] = weighted
            r.slope[b, part, :] = d[part] * feats
            for harmonic in harmonics[order]:
                term = weighted if harmonic is None else weighted * harmonic
                high, low = high_low(term)
                r.terms[row : row + CH, 0:BL] = high.astype(BF16)
                r.terms[row : row + CH, BL : 2 * BL] = low.astype(BF16)
                row += CH
        pick_target = r.to_own[b, 0:AP, :]
        twice = jnp.concatenate([pick_target, pick_target], 1)
        r.moments[...] += dot(r.terms[...], twice, NT)
        return carry

    lax.fori_loop(0, STEPS, step, 0)


def readout(r):
    def moment(i):
        return r.moments[CH * i : CH * (i + 1), :]

    squares = []
    for low, high in ((1, 4), (4, 9)):
        total = moment(low) * moment(low)
        for i in range(low + 1, high):
            total = total + moment(i) * moment(i)
        squares.append(total)
    invariants = jnp.concatenate([moment(0)] + squares, 0)
    mix = r.mix[...]
    mix_t = mix.astype(F32).T.astype(BF16)
    high, low = high_low(invariants)
    mixed = dot(mix_t, high.astype(BF16)) + dot(mix_t, low.astype(BF16))
    head = jnp.broadcast_to(r.head[...].astype(F32), (128, 128)).T
    head = jnp.concatenate([head] * 4, 1)
    h, slope = silu_parts(mixed)
    d_mixed = stack_high_low(head * slope)
    d_inv = dot(jnp.concatenate([mix, mix], 1), d_mixed)
    for i in range(9):
        order = 0 if i == 0 else (1 if i < 4 else 2)
        grad = d_inv[CH * order : CH * (order + 1)]
        if order:
            grad = 2.0 * moment(i) * grad
        high, low = high_low(grad)
        r.grads[CH * i : CH * (i + 1), 0:AP] = high.astype(BF16)
        r.grads[CH * i : CH * (i + 1), AP : 2 * AP] = low.astype(BF16)
    energy = jnp.sum(head * h, axis=0, keepdims=True)[:, :A]
    kinds = r.species[...]
    for k in range(SPECIES):
        energy = energy + jnp.where(kinds == k, r.shift[k], 0.0)
    r.out[0] = energy


def pulls(r):
    def step(b, carry):
        r.back[...] = dot(r.grads[...], r.to_own[b])
        v = r.geom[0:3, span(b)]
        along, across = [], []
        for i in range(9):
            order = 0 if i == 0 else (1 if i < 4 else 2)
            part = slice(CH * order, CH * (order + 1))
            grad = r.back[CH * i : CH * (i + 1), :]
            if order:
                along.append(jnp.sum(r.radial[b, part, :] * grad, axis=0, keepdims=True))
            across.append(jnp.sum(r.slope[b, part, :] * grad, axis=0, keepdims=True))
        x, y, z = 0.5 * v[0:1], 0.5 * v[1:2], 0.5 * v[2:3]
        ax, ay, az, b0, b1, b2, b3, b4 = along
        dq = across[0] + x * across[1] + y * across[2] + z * across[3]
        for harmonic, c in zip(harmonics_of(x, y, z), across[4:]):
            dq = dq + harmonic * c
        gx = ax + ROOT3 * (y * b0 + z * b3 + x * b4) - x * b2
        gy = ay + ROOT3 * (x * b0 + z * b1 - y * b4) - y * b2
        gz = az + ROOT3 * (y * b1 + x * b3) + 2.0 * z * b2
        px = 0.5 * gx + 2.0 * dq * v[0:1]
        py = 0.5 * gy + 2.0 * dq * v[1:2]
        pz = 0.5 * gz + 2.0 * dq * v[2:3]
        pull = jnp.concatenate([px, py, pz, jnp.zeros((5, BL), F32)], 0)
        r.pull[b] = stack_high_low(pull)
        return carry

    lax.fori_loop(0, STEPS, step, 0)


def spread(pull_ref, pick):
    total = None
    for b in range(STEPS):
        part = dot(pull_ref[b], pick(b), NT)
        total = part if total is None else total + part
    return total[:8] + total[8:]


def give_ghosts(r):
    r.ghost[...] = -spread(r.pull, lambda b: r.from_ghost[b])


def own_forces(r):
    return spread(r.pull, lambda b: r.to_own[b, 0:AP, :] - r.from_own[b])


class Refs:
    def __init__(self, names, refs):
        for name, ref in zip(names, refs, strict=True):
            setattr(self, name, ref)


LOADS = {
    "pos": ((3, A), BF16),
    "feat": ((A, CH), BF16),
    "list": ((1, G), jnp.int32),
    "source": ((NB, 1, PB), jnp.int32),
    "target": ((NB, 1, PB), jnp.int32),
    "first": ((NRB, RH), BF16),
    "second": ((RH, RH), BF16),
    "third": ((RH, 3 * CH), BF16),
    "mix": ((3 * CH, CH), BF16),
    "head": ((1, CH), BF16),
    "species": ((1, A), jnp.int32),
}
WORK = {
    "own_table": ((CH + 16, AP), BF16),
    "table": ((CH + 16, GT), BF16),
    "keys": ((GT, BL), KEY),
    "from_own": ((STEPS, AP, BL), BF16),
    "from_ghost": ((STEPS, GT, BL), BF16),
    "to_own": ((STEPS, 2 * AP, BL), BF16),
    "near": ((CH + 8, NP), F32),
    "feats": ((CH, NP), F32),
    "geom": ((8, NP), F32),
    "hidden": ((2, 2 * RH, NP), BF16),
    "radial": ((STEPS, 3 * CH, BL), F32),
    "slope": ((STEPS, 3 * CH, BL), F32),
    "terms": ((9 * CH, 2 * BL), BF16),
    "moments": ((9 * CH, AP), F32),
    "grads": ((9 * CH, 2 * AP), BF16),
    "back": ((9 * CH, BL), F32),
    "pull": ((STEPS, 16, BL), BF16),
    "ghost": ((8, GT), F32),
    "pick": ((GT, A), BF16),
    "sent": ((SENT, CH), BF16),
    "got": ((SENT, CH), BF16),
    "returned": ((26, 8, 128), F32),
}
INPUTS = ["count", "shift"] + ["hbm_" + name for name in LOADS]
NAMES = INPUTS + ["out"] + list(LOADS) + list(WORK)
NAMES += ["load_sem", "send_sem", "recv_sem", "back_send_sem", "back_recv_sem"]


def kernel(*refs):
    r = Refs(NAMES, refs)
    loads = {}
    for i, name in enumerate(LOADS):
        loads[name] = pltpu.make_async_copy(
            getattr(r, "hbm_" + name), getattr(r, name), r.load_sem.at[i]
        )
        loads[name].start()
    barrier = enter()
    for name in ("pos", "feat", "list"):
        loads.pop(name).wait()
    choose(r.pos, r.feat, r.list, r.pick, r.sent)
    pl.semaphore_wait(barrier, 26)
    copies = []
    for i, (slot, rows, row, _) in enumerate(PLACES):
        copies.append(
            pltpu.make_async_remote_copy(
                src_ref=r.sent.at[row : row + rows, :],
                dst_ref=r.got.at[row : row + rows, :],
                send_sem=r.send_sem.at[i],
                recv_sem=r.recv_sem.at[i],
                device_id=neighbour(slot, -1),
                device_id_type=MESH,
            )
        )
        copies[-1].start()
    for copy in loads.values():
        copy.wait()
    prepare(r)
    for copy in copies:
        copy.wait()
    ghost_table(r.got, r.table, r.keys)
    gather(r)
    radial(r)
    scatter(r)
    readout(r)
    pulls(r)
    give_ghosts(r)
    copies = []
    for i, (slot, rows, _, lane) in enumerate(PLACES):
        start = lane // 128 * 128
        copies.append(
            pltpu.make_async_remote_copy(
                src_ref=r.ghost.at[:, start : start + 128],
                dst_ref=r.returned.at[i],
                send_sem=r.back_send_sem.at[i],
                recv_sem=r.back_recv_sem.at[i],
                device_id=neighbour(slot, 1),
                device_id_type=MESH,
            )
        )
        copies[-1].start()
    own = own_forces(r)[:, :A]
    for copy in copies:
        copy.wait()
    tiles = [[] for _ in range(10)]
    for i, place in enumerate(PLACES):
        tiles[place[3] // 128].append(r.returned[i])
    tiles = [group_lanes(members, 128 // len(members)) for members in tiles]
    sums = dot(stack_high_low(jnp.concatenate(tiles, 1)), r.pick[...])
    total = own + sums[:8] + sums[8:]
    for axis in range(3):
        r.out[axis + 1] = total[axis : axis + 1]


def vmem():
    return pl.BlockSpec(memory_space=pltpu.VMEM)


def smem():
    return pl.BlockSpec(memory_space=pltpu.SMEM)


def shape(dims, kind=F32):
    return jax.ShapeDtypeStruct(dims, kind)


def shards(
    positions,
    features,
    species,
    species_shift,
    send_index,
    pair_target,
    pair_source,
    block_count,
    radial_first,
    radial_second,
    radial_third,
    invariant_mix,
    energy_head,
):
    both = pl.pallas_call(
        kernel,
        out_shape=shape((4, 1, A)),
        in_specs=[smem()] * 2 + [pl.BlockSpec(memory_space=pl.ANY)] * len(LOADS),
        out_specs=vmem(),
        scratch_shapes=[pltpu.VMEM(*spec) for spec in LOADS.values()]
        + [pltpu.VMEM(*spec) for spec in WORK.values()]
        + [pltpu.SemaphoreType.DMA((len(LOADS),))]
        + [pltpu.SemaphoreType.DMA((26,))] * 4,
        compiler_params=pltpu.CompilerParams(
            collective_id=0, has_side_effects=True, vmem_limit_bytes=56 * 2**20
        ),
        name="layer",
    )(
        block_count,
        species_shift,
        positions.reshape(3, A),
        jnp.swapaxes(features, 3, 4).reshape(A, CH),
        send_index.reshape(1, G),
        pair_source.reshape(NB, 1, PB),
        pair_target.reshape(NB, 1, PB),
        radial_first,
        radial_second,
        radial_third,
        invariant_mix,
        energy_head.reshape(1, CH),
        species.reshape(1, A),
    )
    return (both[0].reshape(1, 1, 1, A), both[1:].reshape(1, 1, 1, 3, A))


def solution(mesh):
    split = ("gx", "gy", "gz")
    return jax.shard_map(
        shards,
        mesh=mesh,
        in_specs=(
            P(*split, None, None),
            P(*split, None, None),
            P(*split, None),
            P(),
            P(*split, None),
            P(*split, None, None),
            P(*split, None, None),
            P(*split),
            P(),
            P(),
            P(),
            P(),
            P(),
        ),
        out_specs=(P(*split, None), P(*split, None, None)),
        check_vma=False,
    )
```

```python
import functools

import jax
import jax.numpy as jnp
import numpy as np
from jax import lax
from jax.experimental import pallas as pl
from jax.experimental.pallas import tpu as pltpu
from jax.sharding import PartitionSpec as P

A = 432
AP = 512
G = 304
CH = 128
NB = 10
PB = 128
BL = 256
STEPS = NB * PB // BL
NP = NB * PB
RH = 64
NRB = 8
SPECIES = 10
GT = 1280
SENT = 1088
CELL = 2.5
SIDE = 15.0
CUT = 25.0
MID = 152.0
SCALE = 0.15
ROOT3 = 1.7320508075688772

F32 = jnp.float32
BF16 = jnp.bfloat16
MESH = pl.DeviceIdType.MESH
KEY = jnp.int32
NN = (((1,), (0,)), ((), ()))
NT = (((1,), (1,)), ((), ()))


def offset_of(slot):
    return (slot // 9 - 1, slot // 3 % 3 - 1, slot % 3 - 1)


def places():
    by_kind = {1: [], 2: [], 3: []}
    for slot in range(27):
        if slot != 13:
            by_kind[sum(abs(c) for c in offset_of(slot))].append(slot)
    out = []
    for i, slot in enumerate(by_kind[1]):
        out.append((slot, 96, 96 * i, 128 * i))
    for i, slot in enumerate(by_kind[2]):
        out.append((slot, 32, 576 + 32 * i, 768 + 32 * i))
    for i, slot in enumerate(by_kind[3]):
        out.append((slot, 16, 960 + 16 * i, 1152 + 16 * i))
    return out


PLACES = places()


def far_first():
    def way(place):
        x, y, z = offset_of(place[0])
        return -(4 * abs(z) + 2 * abs(y) + abs(x))

    return sorted(enumerate(PLACES), key=lambda item: way(item[1]))


ORDER = far_first()


def dot(a, b, dims=NN):
    return lax.dot_general(a, b, dims, preferred_element_type=F32)


def iota(shape, dim):
    return lax.broadcasted_iota(jnp.int32, shape, dim)


def high_low(x):
    high = x.astype(BF16).astype(F32)
    return high, x - high


def neighbours():
    steps = {}
    for axis, size in (("gx", 4), ("gy", 4), ("gz", 16)):
        me = lax.axis_index(axis)
        steps[axis] = {0: me, 1: lax.rem(me + 1, size), -1: lax.rem(me + size - 1, size)}

    def at(slot, sign):
        offset = offset_of(slot)
        return tuple(steps[axis][sign * o] for axis, o in zip(("gx", "gy", "gz"), offset))

    return at


def enter(at):
    barrier = pltpu.get_barrier_semaphore()
    for _, (slot, *_) in ORDER:
        pl.semaphore_signal(barrier, inc=1, device_id=at(slot, 1), device_id_type=MESH)
    return barrier


def choose(pos_ref, feat_ref, list_ref, pick_ref, send_ref):
    pos = pos_ref[...].astype(F32)
    entry = (iota((A, G), 0) == list_ref[...]).astype(BF16)
    ids = iota((8, G), 1).astype(F32)
    coded = jnp.where(ids < MID, ids - MID, ids - (MID - 1.0))
    code = dot(coded.astype(BF16), entry, NT)
    member = (code[0:1] != 0.0).astype(F32)
    slots = iota((32, A), 0)
    ix = (slots >= 9).astype(jnp.int32) + (slots >= 18).astype(jnp.int32)
    rest = slots - 9 * ix
    iy = (rest >= 3).astype(jnp.int32) + (rest >= 6).astype(jnp.int32)
    iz = rest - 3 * iy
    strict = member
    closed = member
    for axis, index in enumerate((ix, iy, iz)):
        x = pos[axis : axis + 1]
        one = jnp.ones((1, A), F32)
        strict = strict * jnp.where(
            index == 0,
            (x > SIDE - CELL).astype(F32),
            jnp.where(index == 2, (x < CELL).astype(F32), one),
        )
        closed = closed * jnp.where(
            index == 0,
            (x >= SIDE - CELL).astype(F32),
            jnp.where(index == 2, (x <= CELL).astype(F32), one),
        )
    both = jnp.concatenate([strict, closed - strict], 0)
    upper = (iota((A, A), 0) <= iota((A, A), 1)).astype(BF16)
    count = dot(both.astype(BF16), upper)
    total = count[:32, A - 1 : A]
    rank = jnp.where(
        strict > 0.0,
        count[:32] - 1.0,
        jnp.where(closed > 0.0, total + count[32:] - 1.0, -1.0),
    )
    for slot, rows, _, lane in PLACES:
        tall = 128 if rows == 96 else rows
        step = iota((tall, A), 0)
        step = jnp.where(step < rows - 4, step, -2).astype(F32)
        pick_ref[lane : lane + tall, :] = (step == rank[slot : slot + 1]).astype(BF16)
    meta = jnp.concatenate([jnp.zeros((4, A), F32), pos, code[0:1]], 0).astype(BF16)
    feat = feat_ref[...]
    for slot, rows, row, lane in PLACES:
        if rows == 96:
            block = dot(pick_ref[lane : lane + 96, :], feat)
            told = dot(meta, pick_ref[lane : lane + 128, :], NT)
            out = jnp.concatenate([block[:88], block[88:96] + told], 0)
            send_ref[row : row + 96, :] = out.astype(BF16)
    for group in range(4):
        start = 768 + 128 * group
        rows = 32 if group < 3 else 16
        block = dot(pick_ref[start : start + 128, :], feat)
        told = dot(meta, pick_ref[start : start + 128, :], NT)
        pieces = []
        for i in range(128 // rows):
            pieces.append(block[rows * i : rows * i + rows - 8])
            pieces.append(block[rows * i + rows - 8 : rows * (i + 1)] + told)
        row = 576 + 128 * group
        send_ref[row : row + 128, :] = jnp.concatenate(pieces, 0).astype(BF16)


def group_lanes(tiles, width):
    lane = iota(tiles[0].shape, 1)
    out = tiles[0]
    for i in range(1, len(tiles)):
        out = jnp.where(lane >= width * i, tiles[i], out)
    return out


def ghost_table(got_ref, table_ref, key_ref):
    tiles = [[] for _ in range(10)]
    for place in PLACES:
        tiles[place[3] // 128].append(place)
    for t, members in enumerate(tiles):
        width = 128 // len(members)
        row, rows = members[0][2], members[0][1]
        if rows == 96:
            feats = jnp.concatenate(
                [got_ref[row : row + 96, :].astype(F32), jnp.zeros((32, CH), F32)], 0
            )
        else:
            feats = got_ref[row : row + 128, :].astype(F32)
        table_ref[0:CH, 128 * t : 128 * (t + 1)] = feats.T.astype(BF16)
        told, offs = [], []
        for slot, rows, row, _ in members:
            told.append(got_ref[row + rows - 16 : row + rows, :].astype(F32)[8:16])
        told = group_lanes(told, width)
        sub = iota((8, 128), 0)
        for slot, *_ in members:
            o = offset_of(slot)
            offs.append(
                jnp.where(
                    sub == 0,
                    float(o[0]),
                    jnp.where(sub == 1, float(o[1]), jnp.where(sub == 2, float(o[2]), 0.0)),
                )
            )
        offs = group_lanes(offs, width)
        base = group_lanes(
            [jnp.full((8, 128), float(A + G * slot), F32) for slot, *_ in members], width
        )
        table_ref[CH : CH + 16, 128 * t : 128 * (t + 1)] = jnp.concatenate(
            [told, offs], 0
        ).astype(BF16)
        code = told[7:8]
        index = jnp.where(code < 0.0, code + MID, code + (MID - 1.0)) + base[0:1]
        key = jnp.where(code == 0.0, -5.0, index)
        column = jnp.broadcast_to(key, (128, 128)).T.astype(KEY)
        key_ref[128 * t : 128 * (t + 1), :] = jnp.concatenate([column, column], 1)


def silu_parts(z):
    s = 0.5 * jnp.tanh(0.5 * z) + 0.5
    h = z * s
    return h, s + h * (1.0 - s)


def stack_high_low(x):
    return jnp.concatenate(high_low(x), 0).astype(BF16)


def span(b):
    return pl.ds(pl.multiple_of(b * BL, BL), BL)


def pair_rows(ref, b):
    return jnp.concatenate([ref[2 * b], ref[2 * b + 1]], 1)


def twice_across(ref):
    x = ref[...].astype(F32).T
    return jnp.concatenate([x, x], 1).astype(BF16)


def prepare(r):
    r.own_table[...] = jnp.zeros_like(r.own_table)
    feat = r.feat[...].astype(F32).T
    r.own_table[0:CH, 0:A] = feat.astype(BF16)
    pos = jnp.concatenate([r.pos[...].astype(F32), jnp.zeros((13, A), F32)], 0)
    r.own_table[CH : CH + 16, 0:A] = pos.astype(BF16)
    count = r.count[0, 0, 0]

    def near_step(b, carry):
        source = pair_rows(r.source, b)
        target = pair_rows(r.target, b)
        live = 2 * b + (iota((1, BL), 1) >= PB).astype(jnp.int32) < count
        target = jnp.where(live, target, -1)
        atoms = iota((AP, BL), 0)
        pick_own = (atoms == source).astype(BF16)
        pick_target = (atoms == target).astype(BF16)
        r.from_own[b] = pick_own
        r.to_own[b, 0:AP, :] = pick_target
        r.to_own[b, AP : 2 * AP, :] = pick_target
        across = iota((PB, AP), 1)
        for half in range(2):
            part = jnp.broadcast_to(target[:, PB * half : PB * (half + 1)], (PB, PB))
            column = part.astype(F32).T.astype(jnp.int32)
            pick = (across == jnp.concatenate([column] * 4, 1)).astype(BF16)
            r.by_pair[512 * b + PB * half : 512 * b + PB * (half + 1), :] = pick
            r.by_pair[512 * b + BL + PB * half : 512 * b + BL + PB * (half + 1), :] = pick
        near = dot(r.own_table[...], pick_own)
        here = dot(r.own_table[CH : CH + 16, :], pick_target)
        r.near[:, span(b)] = jnp.concatenate([near[:CH], near[CH : CH + 8] - here[:8]], 0)
        return carry

    for b in range(STEPS): near_step(b, 0)


def gather(r):
    def far_step(b, carry):
        source = pair_rows(r.source, b)
        pick_ghost = (r.keys[...] == source.astype(KEY)).astype(BF16)
        r.from_ghost[b] = pick_ghost
        far = dot(r.table[...], pick_ghost)
        near = r.near[:, span(b)]
        r.feats[:, span(b)] = (near[:CH] + far[:CH]) * SCALE
        r.geom[0:3, span(b)] = (
            near[CH : CH + 3] + far[CH + 4 : CH + 7] + SIDE * far[CH + 8 : CH + 11]
        )
        return carry

    lax.fori_loop(0, STEPS, far_step, 0, unroll=True)


def harmonics_of(x, y, z):
    return [
        ROOT3 * x * y,
        ROOT3 * y * z,
        0.5 * (2.0 * z * z - x * x - y * y),
        ROOT3 * x * z,
        0.5 * ROOT3 * (x * x - y * y),
    ]


def radial(r):
    v = r.geom[0:3, :]
    q = v[0:1] * v[0:1] + v[1:2] * v[1:2] + v[2:3] * v[2:3]
    keep = jnp.maximum(1.0 - q / CUT, 0.0)
    envelope = keep * keep
    d_envelope = keep * (-2.0 / CUT)
    centers = iota((NRB, NP), 0).astype(F32) * (CUT / (NRB - 1))
    away = q - centers
    bump = jnp.exp(-(away * away) / CUT)
    basis = bump * envelope
    d_basis = bump * (d_envelope - (2.0 / CUT) * away * envelope)
    first = twice_across(r.first)
    z = dot(first, jnp.concatenate([stack_high_low(basis), stack_high_low(d_basis)], 1))
    h, slope = silu_parts(z[:, :NP])
    d = slope * z[:, NP:]
    second = twice_across(r.second)
    z = dot(second, jnp.concatenate([stack_high_low(h), stack_high_low(d)], 1))
    h, slope = silu_parts(z[:, :NP])
    d = slope * z[:, NP:]
    r.hidden[0] = stack_high_low(h)
    r.hidden[1] = stack_high_low(d)


CHUNKS = ((0, 4), (4, 9))


def scatter(r):
    third = twice_across(r.third)
    v = r.geom[0:3, :]
    ux, uy, uz = 0.5 * v[0:1], 0.5 * v[1:2], 0.5 * v[2:3]
    harmonics = [None, ux, uy, uz] + harmonics_of(ux, uy, uz)
    for first, last in CHUNKS:
        for b in range(STEPS):
            lanes = slice(BL * b, BL * (b + 1))
            for i in range(first, last):
                order = 0 if i == 0 else (1 if i < 4 else 2)
                part = slice(CH * order, CH * (order + 1))
                if i in (0, 1, 4):
                    z = dot(third[part], r.hidden[0, :, lanes])
                    r.radial[b, part, :] = z * r.feats[:, lanes]
                term = r.radial[b, part, :]
                if i:
                    term = term * harmonics[i][:, lanes]
                high, low = high_low(term)
                row = CH * i
                r.terms[row : row + CH, 512 * b : 512 * b + BL] = high.astype(BF16)
                r.terms[row : row + CH, 512 * b + BL : 512 * b + 512] = low.astype(BF16)
        rows = slice(CH * first, CH * last)
        r.moments[rows, :] = dot(r.terms[rows, :], r.by_pair[...])


def readout(r):
    def moment(i):
        return r.moments[CH * i : CH * (i + 1), :]

    squares = []
    for low, high in ((1, 4), (4, 9)):
        total = moment(low) * moment(low)
        for i in range(low + 1, high):
            total = total + moment(i) * moment(i)
        squares.append(total)
    invariants = jnp.concatenate([moment(0)] + squares, 0)
    mix = r.mix[...]
    mix_t = mix.astype(F32).T.astype(BF16)
    high, low = high_low(invariants)
    mixed = dot(mix_t, high.astype(BF16)) + dot(mix_t, low.astype(BF16))
    head = jnp.broadcast_to(r.head[...].astype(F32), (128, 128)).T
    head = jnp.concatenate([head] * 4, 1)
    h, slope = silu_parts(mixed)
    d_mixed = stack_high_low(head * slope)
    d_inv = dot(jnp.concatenate([mix, mix], 1), d_mixed)
    for i in range(9):
        order = 0 if i == 0 else (1 if i < 4 else 2)
        grad = d_inv[CH * order : CH * (order + 1)]
        if order:
            grad = 2.0 * moment(i) * grad
        high, low = high_low(grad)
        r.grads[CH * i : CH * (i + 1), 0:AP] = high.astype(BF16)
        r.grads[CH * i : CH * (i + 1), AP : 2 * AP] = low.astype(BF16)
    energy = jnp.sum(head * h, axis=0, keepdims=True)[:, :A]
    kinds = r.species[...]
    for k in range(SPECIES):
        energy = energy + jnp.where(kinds == k, r.shift[k], 0.0)
    r.out[0] = energy


def pulls(r):
    third = twice_across(r.third)

    def step(b, carry):
        d = dot(third, r.hidden[1, :, span(b)])
        r.back[b] = dot(r.grads[...], r.to_own[b])
        v = r.geom[0:3, span(b)]
        along, across = [], []
        for i in range(9):
            order = 0 if i == 0 else (1 if i < 4 else 2)
            part = slice(CH * order, CH * (order + 1))
            grad = r.back[b, CH * i : CH * (i + 1), :]
            if order:
                along.append(jnp.sum(r.radial[b, part, :] * grad, axis=0, keepdims=True))
            slope = d[part] * r.feats[:, span(b)]
            across.append(jnp.sum(slope * grad, axis=0, keepdims=True))
        x, y, z = 0.5 * v[0:1], 0.5 * v[1:2], 0.5 * v[2:3]
        ax, ay, az, b0, b1, b2, b3, b4 = along
        dq = across[0] + x * across[1] + y * across[2] + z * across[3]
        for harmonic, c in zip(harmonics_of(x, y, z), across[4:]):
            dq = dq + harmonic * c
        gx = ax + ROOT3 * (y * b0 + z * b3 + x * b4) - x * b2
        gy = ay + ROOT3 * (x * b0 + z * b1 - y * b4) - y * b2
        gz = az + ROOT3 * (y * b1 + x * b3) + 2.0 * z * b2
        px = 0.5 * gx + 2.0 * dq * v[0:1]
        py = 0.5 * gy + 2.0 * dq * v[1:2]
        pz = 0.5 * gz + 2.0 * dq * v[2:3]
        pull = jnp.concatenate([px, py, pz, jnp.zeros((5, BL), F32)], 0)
        r.pull[b] = stack_high_low(pull)
        return carry

    for b in range(STEPS): step(b, 0)


def spread(pull_ref, pick):
    total = None
    for b in range(STEPS):
        part = dot(pull_ref[b], pick(b), NT)
        total = part if total is None else total + part
    return total[:8] + total[8:]


def give_ghosts(r):
    r.ghost[...] = -spread(r.pull, lambda b: r.from_ghost[b])


def own_forces(r):
    return spread(r.pull, lambda b: r.to_own[b, 0:AP, :] - r.from_own[b])


class Refs:
    def __init__(self, names, refs):
        for name, ref in zip(names, refs, strict=True):
            setattr(self, name, ref)


LOADS = {
    "pos": ((3, A), BF16),
    "feat": ((A, CH), BF16),
    "list": ((1, G), jnp.int32),
    "source": ((NB, 1, PB), jnp.int32),
    "target": ((NB, 1, PB), jnp.int32),
    "first": ((NRB, RH), BF16),
    "second": ((RH, RH), BF16),
    "third": ((RH, 3 * CH), BF16),
    "mix": ((3 * CH, CH), BF16),
    "head": ((1, CH), BF16),
    "species": ((1, A), jnp.int32),
    "count": ((1, 1, 1), jnp.int32),
    "shift": ((SPECIES,), F32),
}
WORK = {
    "own_table": ((CH + 16, AP), BF16),
    "table": ((CH + 16, GT), BF16),
    "keys": ((GT, BL), KEY),
    "from_own": ((STEPS, AP, BL), BF16),
    "from_ghost": ((STEPS, GT, BL), BF16),
    "to_own": ((STEPS, 2 * AP, BL), BF16),
    "by_pair": ((STEPS * 2 * BL, AP), BF16),
    "near": ((CH + 8, NP), F32),
    "feats": ((CH, NP), F32),
    "geom": ((8, NP), F32),
    "hidden": ((2, 2 * RH, NP), BF16),
    "radial": ((STEPS, 3 * CH, BL), F32),
    "terms": ((9 * CH, STEPS * 2 * BL), BF16),
    "moments": ((9 * CH, AP), F32),
    "grads": ((9 * CH, 2 * AP), BF16),
    "back": ((STEPS, 9 * CH, BL), F32),
    "pull": ((STEPS, 16, BL), BF16),
    "ghost": ((8, GT), F32),
    "pick": ((GT, A), BF16),
    "sent": ((SENT, CH), BF16),
    "got": ((SENT, CH), BF16),
    "returned": ((26, 8, 128), F32),
}
INPUTS = ["hbm_" + name for name in LOADS]
NAMES = INPUTS + ["out"] + list(LOADS) + list(WORK)
NAMES += ["load_sem", "send_sem", "recv_sem", "back_send_sem", "back_recv_sem"]


def kernel(*refs):
    r = Refs(NAMES, refs)
    at = neighbours()
    barrier = enter(at)
    loads = {}
    for i, name in enumerate(LOADS):
        loads[name] = pltpu.make_async_copy(
            getattr(r, "hbm_" + name), getattr(r, name), r.load_sem.at[i]
        )
        loads[name].start()
    for name in ("pos", "feat", "list"):
        loads.pop(name).wait()
    choose(r.pos, r.feat, r.list, r.pick, r.sent)
    pl.semaphore_wait(barrier, 26)
    copies = []
    for i, (slot, rows, row, _) in ORDER:
        copies.append(
            pltpu.make_async_remote_copy(
                src_ref=r.sent.at[row : row + rows, :],
                dst_ref=r.got.at[row : row + rows, :],
                send_sem=r.send_sem.at[i],
                recv_sem=r.recv_sem.at[i],
                device_id=at(slot, -1),
                device_id_type=MESH,
            )
        )
        copies[-1].start()
    for copy in loads.values():
        copy.wait()
    prepare(r)
    for copy in copies:
        copy.wait_recv()
    ghost_table(r.got, r.table, r.keys)
    gather(r)
    radial(r)
    scatter(r)
    readout(r)
    pulls(r)
    give_ghosts(r)
    returns = []
    for i, (slot, rows, _, lane) in ORDER:
        start = lane // 128 * 128
        returns.append(
            pltpu.make_async_remote_copy(
                src_ref=r.ghost.at[:, start : start + 128],
                dst_ref=r.returned.at[i],
                send_sem=r.back_send_sem.at[i],
                recv_sem=r.back_recv_sem.at[i],
                device_id=at(slot, 1),
                device_id_type=MESH,
            )
        )
        returns[-1].start()
    own = own_forces(r)[:, :A]
    for copy in copies:
        copy.wait_send()
    for copy in returns:
        copy.wait_recv()
    tiles = [[] for _ in range(10)]
    for i, place in enumerate(PLACES):
        tiles[place[3] // 128].append(r.returned[i])
    tiles = [group_lanes(members, 128 // len(members)) for members in tiles]
    sums = dot(stack_high_low(jnp.concatenate(tiles, 1)), r.pick[...])
    total = own + sums[:8] + sums[8:]
    for axis in range(3):
        r.out[axis + 1] = total[axis : axis + 1]
    for copy in returns:
        copy.wait_send()


def split_kernel(both_ref, energy_ref, force_ref, sem):
    first = pltpu.make_async_copy(both_ref.at[0:1], energy_ref, sem.at[0])
    second = pltpu.make_async_copy(both_ref.at[1:4], force_ref, sem.at[1])
    first.start()
    second.start()
    first.wait()
    second.wait()


def vmem():
    return pl.BlockSpec(memory_space=pltpu.VMEM)


def shape(dims, kind=F32):
    return jax.ShapeDtypeStruct(dims, kind)


def shards(
    positions,
    features,
    species,
    species_shift,
    send_index,
    pair_target,
    pair_source,
    block_count,
    radial_first,
    radial_second,
    radial_third,
    invariant_mix,
    energy_head,
):
    both = pl.pallas_call(
        kernel,
        out_shape=shape((4, 1, A)),
        in_specs=[pl.BlockSpec(memory_space=pl.ANY)] * len(LOADS),
        out_specs=vmem(),
        scratch_shapes=[
            (pltpu.SMEM if name in ("count", "shift") else pltpu.VMEM)(*spec)
            for name, spec in LOADS.items()
        ]
        + [pltpu.VMEM(*spec) for spec in WORK.values()]
        + [pltpu.SemaphoreType.DMA((len(LOADS),))]
        + [pltpu.SemaphoreType.DMA((26,))] * 4,
        compiler_params=pltpu.CompilerParams(
            collective_id=0, has_side_effects=True, vmem_limit_bytes=56 * 2**20
        ),
        name="layer",
    )(
        positions.reshape(3, A),
        jnp.swapaxes(features, 3, 4).reshape(A, CH),
        send_index.reshape(1, G),
        pair_source.reshape(NB, 1, PB),
        pair_target.reshape(NB, 1, PB),
        radial_first,
        radial_second,
        radial_third,
        invariant_mix,
        energy_head.reshape(1, CH),
        species.reshape(1, A),
        block_count,
        species_shift,
    )
    energies, forces = pl.pallas_call(
        split_kernel,
        out_shape=(shape((1, 1, A)), shape((3, 1, A))),
        in_specs=[pl.BlockSpec(memory_space=pl.ANY)],
        out_specs=(pl.BlockSpec(memory_space=pl.ANY),) * 2,
        scratch_shapes=[pltpu.SemaphoreType.DMA((2,))],
        name="split",
    )(both)
    return (energies.reshape(1, 1, 1, A), forces.reshape(1, 1, 1, 3, A))


def solution(mesh):
    split = ("gx", "gy", "gz")
    return jax.shard_map(
        shards,
        mesh=mesh,
        in_specs=(
            P(*split, None, None),
            P(*split, None, None),
            P(*split, None),
            P(),
            P(*split, None),
            P(*split, None, None),
            P(*split, None, None),
            P(*split),
            P(),
            P(),
            P(),
            P(),
            P(),
        ),
        out_specs=(P(*split, None), P(*split, None, None)),
        check_vma=False,
    )
```

```python
import functools

import jax
import jax.numpy as jnp
import numpy as np
from jax import lax
from jax.experimental import pallas as pl
from jax.experimental.pallas import tpu as pltpu
from jax.sharding import PartitionSpec as P

A = 432
AP = 512
G = 304
CH = 128
NB = 10
PB = 128
BL = 256
STEPS = NB * PB // BL
NP = NB * PB
RH = 64
NRB = 8
SPECIES = 10
GT = 1280
SENT = 1088
CELL = 2.5
SIDE = 15.0
CUT = 25.0
MID = 152.0
SCALE = 0.15
ROOT3 = 1.7320508075688772

F32 = jnp.float32
BF16 = jnp.bfloat16
MESH = pl.DeviceIdType.MESH
NN = (((1,), (0,)), ((), ()))
NT = (((1,), (1,)), ((), ()))


def offset_of(slot):
    return (slot // 9 - 1, slot // 3 % 3 - 1, slot % 3 - 1)


def places():
    out = []
    row, lane = 0, 0
    for far in (False, True):
        for kind, rows, lanes in ((1, 96, 128), (2, 32, 32), (3, 16, 16)):
            for slot in range(27):
                offset = offset_of(slot)
                if sum(abs(c) for c in offset) == kind and (offset[2] != 0) == far:
                    out.append((slot, rows, row, lane))
                    row, lane = row + rows, lane + lanes
    return out


PLACES = places()
HALF = GT // 2
NEAR, FAR = 0, 1


def tiles_of(half):
    tiles = {}
    for i, place in enumerate(PLACES):
        if place[3] // HALF == half:
            tiles.setdefault(place[3] // 128, []).append((i, place))
    return tiles


def far_first():
    def way(place):
        x, y, z = offset_of(place[0])
        return -(4 * abs(z) + 2 * abs(y) + abs(x))

    return sorted(enumerate(PLACES), key=lambda item: way(item[1]))


ORDER = far_first()


def dot(a, b, dims=NN):
    return lax.dot_general(a, b, dims, preferred_element_type=F32)


def iota(shape, dim):
    return lax.broadcasted_iota(jnp.int32, shape, dim)


def high_low(x):
    high = x.astype(BF16).astype(F32)
    return high, x - high


def neighbours():
    steps = {}
    for axis, size in (("gx", 4), ("gy", 4), ("gz", 16)):
        me = lax.axis_index(axis)
        steps[axis] = {0: me, 1: lax.rem(me + 1, size), -1: lax.rem(me + size - 1, size)}

    def at(slot, sign):
        offset = offset_of(slot)
        return tuple(steps[axis][sign * o] for axis, o in zip(("gx", "gy", "gz"), offset))

    return at


def enter(at):
    barrier = pltpu.get_barrier_semaphore()
    for _, (slot, *_) in ORDER:
        pl.semaphore_signal(barrier, inc=1, device_id=at(slot, 1), device_id_type=MESH)
    return barrier


def choose(pos_ref, feat_ref, list_ref, pick_ref, send_ref, send):
    pos = pos_ref[...].astype(F32)
    entry = (iota((A, G), 0) == list_ref[...]).astype(BF16)
    ids = iota((8, G), 1).astype(F32)
    coded = jnp.where(ids < MID, ids - MID, ids - (MID - 1.0))
    code = dot(coded.astype(BF16), entry, NT)
    member = (code[0:1] != 0.0).astype(F32)
    slots = iota((32, A), 0)
    ix = (slots >= 9).astype(jnp.int32) + (slots >= 18).astype(jnp.int32)
    rest = slots - 9 * ix
    iy = (rest >= 3).astype(jnp.int32) + (rest >= 6).astype(jnp.int32)
    iz = rest - 3 * iy
    strict = member
    closed = member
    for axis, index in enumerate((ix, iy, iz)):
        x = pos[axis : axis + 1]
        one = jnp.ones((1, A), F32)
        strict = strict * jnp.where(
            index == 0,
            (x > SIDE - CELL).astype(F32),
            jnp.where(index == 2, (x < CELL).astype(F32), one),
        )
        closed = closed * jnp.where(
            index == 0,
            (x >= SIDE - CELL).astype(F32),
            jnp.where(index == 2, (x <= CELL).astype(F32), one),
        )
    both = jnp.concatenate([strict, closed - strict], 0)
    upper = (iota((A, A), 0) <= iota((A, A), 1)).astype(BF16)
    count = dot(both.astype(BF16), upper)
    total = count[:32, A - 1 : A]
    rank = jnp.where(
        strict > 0.0,
        count[:32] - 1.0,
        jnp.where(closed > 0.0, total + count[32:] - 1.0, -1.0),
    )
    meta = jnp.concatenate([jnp.zeros((4, A), F32), pos, code[0:1]], 0).astype(BF16)
    feat = feat_ref[...]
    for half in (FAR, NEAR):
        for t, members in tiles_of(half).items():
            tile = slice(128 * t, 128 * (t + 1))
            rows = members[0][1][1]
            for _, (slot, _, _, lane) in members:
                tall = 128 if rows == 96 else rows
                step = iota((tall, A), 0)
                step = jnp.where(step < rows - 4, step, -2).astype(F32)
                pick_ref[lane : lane + tall, :] = (step == rank[slot : slot + 1]).astype(BF16)
            block = dot(pick_ref[tile, :], feat)
            told = dot(meta, pick_ref[tile, :], NT)
            pieces = []
            for i in range(len(members)):
                pieces.append(block[rows * i : rows * i + rows - 8])
                pieces.append(block[rows * i + rows - 8 : rows * (i + 1)] + told)
            row = members[0][1][2]
            send_ref[row : row + rows * len(members), :] = jnp.concatenate(pieces, 0).astype(BF16)
        send(half)


def group_lanes(tiles, width):
    lane = iota(tiles[0].shape, 1)
    out = tiles[0]
    for i in range(1, len(tiles)):
        out = jnp.where(lane >= width * i, tiles[i], out)
    return out


def ghost_table(got_ref, table_ref, key_ref, half):
    for t, members in tiles_of(half).items():
        members = [place for _, place in members]
        width = 128 // len(members)
        row, rows = members[0][2], members[0][1]
        if rows == 96:
            feats = jnp.concatenate(
                [got_ref[row : row + 96, :].astype(F32), jnp.zeros((32, CH), F32)], 0
            )
        else:
            feats = got_ref[row : row + 128, :].astype(F32)
        table_ref[0:CH, 128 * t : 128 * (t + 1)] = feats.T.astype(BF16)
        told, offs = [], []
        for slot, rows, row, _ in members:
            told.append(got_ref[row + rows - 16 : row + rows, :].astype(F32)[8:16])
        told = group_lanes(told, width)
        sub = iota((8, 128), 0)
        for slot, *_ in members:
            o = offset_of(slot)
            offs.append(
                jnp.where(
                    sub == 4,
                    float(o[0]),
                    jnp.where(sub == 5, float(o[1]), jnp.where(sub == 6, float(o[2]), 0.0)),
                )
            )
        offs = group_lanes(offs, width)
        base = group_lanes(
            [jnp.full((8, 128), float(A + G * slot), F32) for slot, *_ in members], width
        )
        table_ref[CH : CH + 16, 128 * t : 128 * (t + 1)] = jnp.concatenate(
            [told, offs], 0
        ).astype(BF16)
        code = told[7:8]
        index = jnp.where(code < 0.0, code + MID, code + (MID - 1.0)) + base[0:1]
        key = jnp.where(code == 0.0, -5.0, index)
        column = jnp.broadcast_to(key, (128, 128)).T.astype(jnp.int32)
        key_ref[128 * t : 128 * (t + 1), :] = jnp.concatenate([column, column], 1)


def silu_parts(z):
    s = 0.5 * jnp.tanh(0.5 * z) + 0.5
    h = z * s
    return h, s + h * (1.0 - s)


def stack_high_low(x):
    return jnp.concatenate(high_low(x), 0).astype(BF16)


def span(b):
    return slice(BL * b, BL * (b + 1))


def pair_rows(ref, b):
    return jnp.concatenate([ref[2 * b], ref[2 * b + 1]], 1)


def twice_across(ref):
    x = ref[...].astype(F32).T
    return jnp.concatenate([x, x], 1).astype(BF16)


def prepare(r):
    r.own_table[...] = jnp.zeros_like(r.own_table)
    feat = r.feat[...].astype(F32).T
    r.own_table[0:CH, 0:A] = feat.astype(BF16)
    none = jnp.zeros((4, A), F32)
    pos = jnp.concatenate([none, r.pos[...].astype(F32), none, none, none[:1]], 0)
    r.own_table[CH : CH + 16, 0:A] = pos.astype(BF16)
    count = r.count[0, 0, 0]

    for b in range(STEPS):
        source = pair_rows(r.source, b)
        target = pair_rows(r.target, b)
        live = 2 * b + (iota((1, BL), 1) >= PB).astype(jnp.int32) < count
        target = jnp.where(live, target, -1)
        atoms = iota((AP, BL), 0)
        pick_own = (atoms == source).astype(BF16)
        pick_target = (atoms == target).astype(BF16)
        r.from_own[b] = pick_own
        r.to_own[b, 0:AP, :] = pick_target
        r.to_own[b, AP : 2 * AP, :] = pick_target
        across = iota((PB, AP), 1)
        for half in range(2):
            part = jnp.broadcast_to(target[:, PB * half : PB * (half + 1)], (PB, PB))
            column = part.astype(F32).T.astype(jnp.int32)
            pick = (across == jnp.concatenate([column] * 4, 1)).astype(BF16)
            r.by_pair[512 * b + PB * half : 512 * b + PB * (half + 1), :] = pick
            r.by_pair[512 * b + BL + PB * half : 512 * b + BL + PB * (half + 1), :] = pick
        near = dot(r.own_table[...], pick_own)
        here = dot(r.own_table[CH : CH + 16, :], pick_target)
        r.near[:, span(b)] = jnp.concatenate([near[:CH], near[CH : CH + 8] - here[:8]], 0)


def gather(r, half):
    rows = slice(HALF * half, HALF * (half + 1))
    for b in range(STEPS):
        lanes = span(b)
        pick_ghost = (r.keys[rows, :] == pair_rows(r.source, b)).astype(BF16)
        r.from_ghost[b, rows, :] = pick_ghost
        found = dot(r.table[:, rows], pick_ghost)
        feats = r.near[:CH, lanes] + found[:CH]
        place = r.near[CH : CH + 8, lanes] + found[CH : CH + 8] + SIDE * found[CH + 8 : CH + 16]
        if half == NEAR:
            r.near[:CH, lanes] = feats
            r.near[CH : CH + 8, lanes] = place
        else:
            r.feats[:, lanes] = feats * SCALE
            r.geom[:, lanes] = place


def harmonics_of(x, y, z):
    return [
        ROOT3 * x * y,
        ROOT3 * y * z,
        0.5 * (2.0 * z * z - x * x - y * y),
        ROOT3 * x * z,
        0.5 * ROOT3 * (x * x - y * y),
    ]


def radial(r):
    v = r.geom[4:7, :]
    q = v[0:1] * v[0:1] + v[1:2] * v[1:2] + v[2:3] * v[2:3]
    keep = jnp.maximum(1.0 - q / CUT, 0.0)
    envelope = keep * keep
    d_envelope = keep * (-2.0 / CUT)
    centers = iota((NRB, NP), 0).astype(F32) * (CUT / (NRB - 1))
    away = q - centers
    bump = jnp.exp(-(away * away) / CUT)
    basis = bump * envelope
    d_basis = bump * (d_envelope - (2.0 / CUT) * away * envelope)
    first = twice_across(r.first)
    z = dot(first, jnp.concatenate([stack_high_low(basis), stack_high_low(d_basis)], 1))
    h, slope = silu_parts(z[:, :NP])
    d = slope * z[:, NP:]
    second = twice_across(r.second)
    z = dot(second, jnp.concatenate([stack_high_low(h), stack_high_low(d)], 1))
    h, slope = silu_parts(z[:, :NP])
    d = slope * z[:, NP:]
    r.hidden[0] = stack_high_low(h)
    r.hidden[1] = stack_high_low(d)


CHUNKS = ((0, 4), (4, 9))


def scatter(r):
    third = twice_across(r.third)
    v = r.geom[4:7, :]
    ux, uy, uz = 0.5 * v[0:1], 0.5 * v[1:2], 0.5 * v[2:3]
    harmonics = [None, ux, uy, uz] + harmonics_of(ux, uy, uz)
    for first, last in CHUNKS:
        for b in range(STEPS):
            lanes = slice(BL * b, BL * (b + 1))
            for i in range(first, last):
                order = 0 if i == 0 else (1 if i < 4 else 2)
                part = slice(CH * order, CH * (order + 1))
                if i in (0, 1, 4):
                    z = dot(third[part], r.hidden[0, :, lanes])
                    r.radial[b, part, :] = z * r.feats[:, lanes]
                    z = dot(third[part], r.hidden[1, :, lanes])
                    r.slope[b, part, :] = z * r.feats[:, lanes]
                term = r.radial[b, part, :]
                if i:
                    term = term * harmonics[i][:, lanes]
                high, low = high_low(term)
                row = CH * i
                r.terms[row : row + CH, 512 * b : 512 * b + BL] = high.astype(BF16)
                r.terms[row : row + CH, 512 * b + BL : 512 * b + 512] = low.astype(BF16)
        rows = slice(CH * first, CH * last)
        r.moments[rows, :] = dot(r.terms[rows, :], r.by_pair[...])


def readout(r):
    def moment(i):
        return r.moments[CH * i : CH * (i + 1), :]

    squares = []
    for low, high in ((1, 4), (4, 9)):
        total = moment(low) * moment(low)
        for i in range(low + 1, high):
            total = total + moment(i) * moment(i)
        squares.append(total)
    invariants = jnp.concatenate([moment(0)] + squares, 0)
    mix = r.mix[...]
    mix_t = mix.astype(F32).T.astype(BF16)
    high, low = high_low(invariants)
    mixed = dot(mix_t, high.astype(BF16)) + dot(mix_t, low.astype(BF16))
    head = jnp.broadcast_to(r.head[...].astype(F32), (128, 128)).T
    head = jnp.concatenate([head] * 4, 1)
    h, slope = silu_parts(mixed)
    d_mixed = stack_high_low(head * slope)
    d_inv = dot(jnp.concatenate([mix, mix], 1), d_mixed)
    for i in range(9):
        order = 0 if i == 0 else (1 if i < 4 else 2)
        grad = d_inv[CH * order : CH * (order + 1)]
        if order:
            grad = 2.0 * moment(i) * grad
        high, low = high_low(grad)
        r.grads[CH * i : CH * (i + 1), 0:AP] = high.astype(BF16)
        r.grads[CH * i : CH * (i + 1), AP : 2 * AP] = low.astype(BF16)
    energy = jnp.sum(head * h, axis=0, keepdims=True)[:, :A]
    kinds = r.species[...]
    for k in range(SPECIES):
        energy = energy + jnp.where(kinds == k, r.shift[k], 0.0)
    r.out[0] = energy


def pulls(r):
    for b in range(STEPS):
        r.back[b] = dot(r.grads[...], r.to_own[b])
        v = r.geom[4:7, span(b)]
        along, across = [], []
        for i in range(9):
            order = 0 if i == 0 else (1 if i < 4 else 2)
            part = slice(CH * order, CH * (order + 1))
            grad = r.back[b, CH * i : CH * (i + 1), :]
            if order:
                along.append(jnp.sum(r.radial[b, part, :] * grad, axis=0, keepdims=True))
            slope = r.slope[b, part, :]
            across.append(jnp.sum(slope * grad, axis=0, keepdims=True))
        x, y, z = 0.5 * v[0:1], 0.5 * v[1:2], 0.5 * v[2:3]
        ax, ay, az, b0, b1, b2, b3, b4 = along
        dq = across[0] + x * across[1] + y * across[2] + z * across[3]
        for harmonic, c in zip(harmonics_of(x, y, z), across[4:]):
            dq = dq + harmonic * c
        gx = ax + ROOT3 * (y * b0 + z * b3 + x * b4) - x * b2
        gy = ay + ROOT3 * (x * b0 + z * b1 - y * b4) - y * b2
        gz = az + ROOT3 * (y * b1 + x * b3) + 2.0 * z * b2
        px = 0.5 * gx + 2.0 * dq * v[0:1]
        py = 0.5 * gy + 2.0 * dq * v[1:2]
        pz = 0.5 * gz + 2.0 * dq * v[2:3]
        pull = jnp.concatenate([px, py, pz, jnp.zeros((5, BL), F32)], 0)
        r.pull[b] = stack_high_low(pull)


def spread(pull_ref, pick):
    total = None
    for b in range(STEPS):
        part = dot(pull_ref[b], pick(b), NT)
        total = part if total is None else total + part
    return total[:8] + total[8:]


def give_ghosts(r, half):
    rows = slice(HALF * half, HALF * (half + 1))
    r.ghost[:, rows] = -spread(r.pull, lambda b: r.from_ghost[b, rows, :])


def own_forces(r):
    return spread(r.pull, lambda b: r.to_own[b, 0:AP, :] - r.from_own[b])


class Refs:
    def __init__(self, names, refs):
        for name, ref in zip(names, refs, strict=True):
            setattr(self, name, ref)


LOADS = {
    "pos": ((3, A), BF16),
    "feat": ((A, CH), BF16),
    "list": ((1, G), jnp.int32),
    "source": ((NB, 1, PB), jnp.int32),
    "target": ((NB, 1, PB), jnp.int32),
    "first": ((NRB, RH), BF16),
    "second": ((RH, RH), BF16),
    "third": ((RH, 3 * CH), BF16),
    "mix": ((3 * CH, CH), BF16),
    "head": ((1, CH), BF16),
    "species": ((1, A), jnp.int32),
    "count": ((1, 1, 1), jnp.int32),
    "shift": ((SPECIES,), F32),
}
WORK = {
    "own_table": ((CH + 16, AP), BF16),
    "table": ((CH + 16, GT), BF16),
    "keys": ((GT, BL), jnp.int32),
    "from_own": ((STEPS, AP, BL), BF16),
    "from_ghost": ((STEPS, GT, BL), BF16),
    "to_own": ((STEPS, 2 * AP, BL), BF16),
    "by_pair": ((STEPS * 2 * BL, AP), BF16),
    "near": ((CH + 8, NP), F32),
    "feats": ((CH, NP), F32),
    "geom": ((8, NP), F32),
    "hidden": ((2, 2 * RH, NP), BF16),
    "radial": ((STEPS, 3 * CH, BL), F32),
    "slope": ((STEPS, 3 * CH, BL), F32),
    "terms": ((9 * CH, STEPS * 2 * BL), BF16),
    "moments": ((9 * CH, AP), F32),
    "grads": ((9 * CH, 2 * AP), BF16),
    "back": ((STEPS, 9 * CH, BL), F32),
    "pull": ((STEPS, 16, BL), BF16),
    "ghost": ((8, GT), F32),
    "pick": ((GT, A), BF16),
    "sent": ((SENT, CH), BF16),
    "got": ((SENT, CH), BF16),
    "returned": ((26, 8, 128), F32),
}
INPUTS = ["hbm_" + name for name in LOADS]
NAMES = INPUTS + ["out"] + list(LOADS) + list(WORK)
NAMES += ["load_sem", "send_sem", "recv_sem", "back_send_sem", "back_recv_sem"]


def kernel(*refs):
    r = Refs(NAMES, refs)
    at = neighbours()
    barrier = enter(at)
    loads = {}
    for i, name in enumerate(LOADS):
        loads[name] = pltpu.make_async_copy(
            getattr(r, "hbm_" + name), getattr(r, name), r.load_sem.at[i]
        )
        loads[name].start()
    for name in ("pos", "feat", "list"):
        loads.pop(name).wait()
    copies = {}

    def send(half):
        if half == FAR:
            pl.semaphore_wait(barrier, 26)
        for i, (slot, rows, row, lane) in ORDER:
            if lane // HALF != half:
                continue
            copies[i] = pltpu.make_async_remote_copy(
                src_ref=r.sent.at[row : row + rows, :],
                dst_ref=r.got.at[row : row + rows, :],
                send_sem=r.send_sem.at[i],
                recv_sem=r.recv_sem.at[i],
                device_id=at(slot, -1),
                device_id_type=MESH,
            )
            copies[i].start()

    choose(r.pos, r.feat, r.list, r.pick, r.sent, send)
    for copy in loads.values():
        copy.wait()
    prepare(r)
    for half in (NEAR, FAR):
        for members in tiles_of(half).values():
            for i, _ in members:
                copies[i].wait_recv()
        ghost_table(r.got, r.table, r.keys, half)
        gather(r, half)
    radial(r)
    scatter(r)
    readout(r)
    pulls(r)
    returns = {}
    for half in (FAR, NEAR):
        give_ghosts(r, half)
        for i, (slot, rows, _, lane) in ORDER:
            if lane // HALF != half:
                continue
            start = lane // 128 * 128
            returns[i] = pltpu.make_async_remote_copy(
                src_ref=r.ghost.at[:, start : start + 128],
                dst_ref=r.returned.at[i],
                send_sem=r.back_send_sem.at[i],
                recv_sem=r.back_recv_sem.at[i],
                device_id=at(slot, 1),
                device_id_type=MESH,
            )
            returns[i].start()
    total = own_forces(r)[:, :A]
    for copy in copies.values():
        copy.wait_send()
    for half in (NEAR, FAR):
        tiles = []
        for members in tiles_of(half).values():
            for i, _ in members:
                returns[i].wait_recv()
            got = [r.returned[i] for i, _ in members]
            tiles.append(group_lanes(got, 128 // len(members)))
        got = stack_high_low(jnp.concatenate(tiles, 1))
        sums = dot(got, r.pick[HALF * half : HALF * (half + 1), :])
        total = total + sums[:8] + sums[8:]
    for axis in range(3):
        r.out[axis + 1] = total[axis : axis + 1]
    for copy in returns.values():
        copy.wait_send()


def split_kernel(both_ref, energy_ref, force_ref, sem):
    first = pltpu.make_async_copy(both_ref.at[0:1], energy_ref, sem.at[0])
    second = pltpu.make_async_copy(both_ref.at[1:4], force_ref, sem.at[1])
    first.start()
    second.start()
    first.wait()
    second.wait()


def vmem():
    return pl.BlockSpec(memory_space=pltpu.VMEM)


def shape(dims, kind=F32):
    return jax.ShapeDtypeStruct(dims, kind)


def shards(
    positions,
    features,
    species,
    species_shift,
    send_index,
    pair_target,
    pair_source,
    block_count,
    radial_first,
    radial_second,
    radial_third,
    invariant_mix,
    energy_head,
):
    both = pl.pallas_call(
        kernel,
        out_shape=pltpu.VMEM((4, 1, A), F32),
        in_specs=[pl.BlockSpec(memory_space=pl.ANY)] * len(LOADS),
        out_specs=vmem(),
        scratch_shapes=[
            (pltpu.SMEM if name in ("count", "shift") else pltpu.VMEM)(*spec)
            for name, spec in LOADS.items()
        ]
        + [pltpu.VMEM(*spec) for spec in WORK.values()]
        + [pltpu.SemaphoreType.DMA((len(LOADS),))]
        + [pltpu.SemaphoreType.DMA((26,))] * 4,
        compiler_params=pltpu.CompilerParams(
            collective_id=0, has_side_effects=True, vmem_limit_bytes=56 * 2**20
        ),
        name="layer",
    )(
        positions.reshape(3, A),
        jnp.swapaxes(features, 3, 4).reshape(A, CH),
        send_index.reshape(1, G),
        pair_source.reshape(NB, 1, PB),
        pair_target.reshape(NB, 1, PB),
        radial_first,
        radial_second,
        radial_third,
        invariant_mix,
        energy_head.reshape(1, CH),
        species.reshape(1, A),
        block_count,
        species_shift,
    )
    energies, forces = pl.pallas_call(
        split_kernel,
        out_shape=(shape((1, 1, A)), shape((3, 1, A))),
        in_specs=[vmem()],
        out_specs=(pl.BlockSpec(memory_space=pl.ANY),) * 2,
        scratch_shapes=[pltpu.SemaphoreType.DMA((2,))],
        compiler_params=pltpu.CompilerParams(vmem_limit_bytes=2**20),
        name="split",
    )(both)
    return (energies.reshape(1, 1, 1, A), forces.reshape(1, 1, 1, 3, A))


def solution(mesh):
    split = ("gx", "gy", "gz")
    return jax.shard_map(
        shards,
        mesh=mesh,
        in_specs=(
            P(*split, None, None),
            P(*split, None, None),
            P(*split, None),
            P(),
            P(*split, None),
            P(*split, None, None),
            P(*split, None, None),
            P(*split),
            P(),
            P(),
            P(),
            P(),
            P(),
        ),
        out_specs=(P(*split, None), P(*split, None, None)),
        check_vma=False,
    )
```

```python
import functools

import jax
import jax.numpy as jnp
import numpy as np
from jax import lax
from jax.experimental import pallas as pl
from jax.experimental.pallas import tpu as pltpu
from jax.sharding import PartitionSpec as P

A = 432
AP = 512
G = 304
CH = 128
NB = 10
PB = 128
BL = 256
STEPS = NB * PB // BL
NP = NB * PB
RH = 64
NRB = 8
SPECIES = 10
GT = 1280
SENT = 1088
CELL = 2.5
SIDE = 15.0
CUT = 25.0
MID = 152.0
SCALE = 0.15
ROOT3 = 1.7320508075688772

F32 = jnp.float32
BF16 = jnp.bfloat16
MESH = pl.DeviceIdType.MESH
NN = (((1,), (0,)), ((), ()))
NT = (((1,), (1,)), ((), ()))


def offset_of(slot):
    return (slot // 9 - 1, slot // 3 % 3 - 1, slot % 3 - 1)


def places():
    out = []
    row, lane = 0, 0
    for far in (False, True):
        for kind, rows, lanes in ((1, 96, 128), (2, 32, 32), (3, 16, 16)):
            for slot in range(27):
                offset = offset_of(slot)
                if sum(abs(c) for c in offset) == kind and (offset[2] != 0) == far:
                    out.append((slot, rows, row, lane))
                    row, lane = row + rows, lane + lanes
    return out


PLACES = places()
HALF = GT // 2
NEAR, FAR = 0, 1


def tiles_of(half):
    tiles = {}
    for i, place in enumerate(PLACES):
        if place[3] // HALF == half:
            tiles.setdefault(place[3] // 128, []).append((i, place))
    return tiles


def far_first():
    def way(place):
        x, y, z = offset_of(place[0])
        return -(4 * abs(z) + 2 * abs(y) + abs(x))

    return sorted(enumerate(PLACES), key=lambda item: way(item[1]))


ORDER = far_first()


def dot(a, b, dims=NN):
    return lax.dot_general(a, b, dims, preferred_element_type=F32)


def iota(shape, dim):
    return lax.broadcasted_iota(jnp.int32, shape, dim)


def high_low(x):
    high = x.astype(BF16).astype(F32)
    return high, x - high


def neighbours():
    steps = {}
    for axis, size in (("gx", 4), ("gy", 4), ("gz", 16)):
        me = lax.axis_index(axis)
        steps[axis] = {0: me, 1: lax.rem(me + 1, size), -1: lax.rem(me + size - 1, size)}

    def at(slot, sign):
        offset = offset_of(slot)
        return tuple(steps[axis][sign * o] for axis, o in zip(("gx", "gy", "gz"), offset))

    return at


def enter(at):
    barrier = pltpu.get_barrier_semaphore()
    for _, (slot, *_) in ORDER:
        pl.semaphore_signal(barrier, inc=1, device_id=at(slot, 1), device_id_type=MESH)
    return barrier


def choose(pos_ref, feat_ref, list_ref, upper_ref, pick_ref, send_ref, send):
    pos = pos_ref[...].astype(F32)
    entry = (iota((A, G), 0) == list_ref[...]).astype(BF16)
    ids = iota((8, G), 1).astype(F32)
    coded = jnp.where(ids < MID, ids - MID, ids - (MID - 1.0))
    code = dot(coded.astype(BF16), entry, NT)
    member = (code[0:1] != 0.0).astype(F32)
    slots = iota((32, A), 0)
    ix = (slots >= 9).astype(jnp.int32) + (slots >= 18).astype(jnp.int32)
    rest = slots - 9 * ix
    iy = (rest >= 3).astype(jnp.int32) + (rest >= 6).astype(jnp.int32)
    iz = rest - 3 * iy
    strict = member
    closed = member
    for axis, index in enumerate((ix, iy, iz)):
        x = pos[axis : axis + 1]
        one = jnp.ones((1, A), F32)
        strict = strict * jnp.where(
            index == 0,
            (x > SIDE - CELL).astype(F32),
            jnp.where(index == 2, (x < CELL).astype(F32), one),
        )
        closed = closed * jnp.where(
            index == 0,
            (x >= SIDE - CELL).astype(F32),
            jnp.where(index == 2, (x <= CELL).astype(F32), one),
        )
    both = jnp.concatenate([strict, closed - strict], 0)
    count = dot(both.astype(BF16), upper_ref[...])
    total = count[:32, A - 1 : A]
    rank = jnp.where(
        strict > 0.0,
        count[:32] - 1.0,
        jnp.where(closed > 0.0, total + count[32:] - 1.0, -1.0),
    )
    meta = jnp.concatenate([jnp.zeros((4, A), F32), pos, code[0:1]], 0).astype(BF16)
    feat = feat_ref[...]
    for half in (FAR, NEAR):
        for t, members in tiles_of(half).items():
            tile = slice(128 * t, 128 * (t + 1))
            rows = members[0][1][1]
            for _, (slot, _, _, lane) in members:
                tall = 128 if rows == 96 else rows
                step = iota((tall, A), 0)
                step = jnp.where(step < rows - 4, step, -2).astype(F32)
                pick_ref[lane : lane + tall, :] = (step == rank[slot : slot + 1]).astype(BF16)
            block = dot(pick_ref[tile, :], feat)
            told = dot(meta, pick_ref[tile, :], NT)
            pieces = []
            for i in range(len(members)):
                pieces.append(block[rows * i : rows * i + rows - 8])
                pieces.append(block[rows * i + rows - 8 : rows * (i + 1)] + told)
            row = members[0][1][2]
            send_ref[row : row + rows * len(members), :] = jnp.concatenate(pieces, 0).astype(BF16)
        send(half)


def group_lanes(tiles, width):
    lane = iota(tiles[0].shape, 1)
    out = tiles[0]
    for i in range(1, len(tiles)):
        out = jnp.where(lane >= width * i, tiles[i], out)
    return out


def ghost_table(got_ref, table_ref, key_ref, half):
    for t, members in tiles_of(half).items():
        members = [place for _, place in members]
        width = 128 // len(members)
        row, rows = members[0][2], members[0][1]
        if rows == 96:
            feats = jnp.concatenate(
                [got_ref[row : row + 96, :].astype(F32), jnp.zeros((32, CH), F32)], 0
            )
        else:
            feats = got_ref[row : row + 128, :].astype(F32)
        table_ref[0:CH, 128 * t : 128 * (t + 1)] = feats.T.astype(BF16)
        told, offs = [], []
        for slot, rows, row, _ in members:
            told.append(got_ref[row + rows - 16 : row + rows, :].astype(F32)[8:16])
        told = group_lanes(told, width)
        sub = iota((8, 128), 0)
        for slot, *_ in members:
            o = offset_of(slot)
            offs.append(
                jnp.where(
                    sub == 4,
                    float(o[0]),
                    jnp.where(sub == 5, float(o[1]), jnp.where(sub == 6, float(o[2]), 0.0)),
                )
            )
        offs = group_lanes(offs, width)
        base = group_lanes(
            [jnp.full((8, 128), float(A + G * slot), F32) for slot, *_ in members], width
        )
        table_ref[CH : CH + 16, 128 * t : 128 * (t + 1)] = jnp.concatenate(
            [told, offs], 0
        ).astype(BF16)
        code = told[7:8]
        index = jnp.where(code < 0.0, code + MID, code + (MID - 1.0)) + base[0:1]
        key = jnp.where(code == 0.0, -5.0, index)
        column = jnp.broadcast_to(key, (128, 128)).T.astype(jnp.int32)
        key_ref[128 * t : 128 * (t + 1), :] = jnp.concatenate([column, column], 1)


def silu_parts(z):
    s = 0.5 * jnp.tanh(0.5 * z) + 0.5
    h = z * s
    return h, s + h * (1.0 - s)


def stack_high_low(x):
    return jnp.concatenate(high_low(x), 0).astype(BF16)


def span(b):
    return slice(BL * b, BL * (b + 1))


def pair_rows(ref, b):
    return jnp.concatenate([ref[2 * b], ref[2 * b + 1]], 1)


def twice_across(ref):
    x = ref[...].astype(F32).T
    return jnp.concatenate([x, x], 1).astype(BF16)


def prepare(r):
    r.own_table[...] = jnp.zeros_like(r.own_table)
    feat = r.feat[...].astype(F32).T
    r.own_table[0:CH, 0:A] = feat.astype(BF16)
    none = jnp.zeros((4, A), F32)
    pos = jnp.concatenate([none, r.pos[...].astype(F32), none, none, none[:1]], 0)
    r.own_table[CH : CH + 16, 0:A] = pos.astype(BF16)
    r.first_t[...] = twice_across(r.first)
    r.second_t[...] = twice_across(r.second)
    r.third_t[...] = twice_across(r.third)
    mix = r.mix[...]
    r.mix_t[...] = mix.astype(F32).T.astype(BF16)
    r.mix_two[...] = jnp.concatenate([mix, mix], 1)
    head = jnp.broadcast_to(r.head[...].astype(F32), (128, 128)).T
    r.head_t[...] = jnp.concatenate([head] * 4, 1)
    kinds = r.species[...]
    base = jnp.zeros((1, A), F32)
    for k in range(SPECIES):
        base = base + jnp.where(kinds == k, r.shift[k], 0.0)
    r.base[...] = base
    count = r.count[0, 0, 0]

    for b in range(STEPS):
        source = pair_rows(r.source, b)
        target = pair_rows(r.target, b)
        live = 2 * b + (iota((1, BL), 1) >= PB).astype(jnp.int32) < count
        target = jnp.where(live, target, -1)
        atoms = iota((AP, BL), 0)
        pick_own = (atoms == source).astype(BF16)
        pick_target = (atoms == target).astype(BF16)
        r.from_own[b] = pick_own
        r.to_own[b, 0:AP, :] = pick_target
        r.to_own[b, AP : 2 * AP, :] = pick_target
        across = iota((PB, AP), 1)
        for half in range(2):
            part = jnp.broadcast_to(target[:, PB * half : PB * (half + 1)], (PB, PB))
            column = part.astype(F32).T.astype(jnp.int32)
            pick = (across == jnp.concatenate([column] * 4, 1)).astype(BF16)
            r.by_pair[512 * b + PB * half : 512 * b + PB * (half + 1), :] = pick
            r.by_pair[512 * b + BL + PB * half : 512 * b + BL + PB * (half + 1), :] = pick
        near = dot(r.own_table[...], pick_own)
        here = dot(r.own_table[CH : CH + 16, :], pick_target)
        r.near[:, span(b)] = jnp.concatenate([near[:CH], near[CH : CH + 8] - here[:8]], 0)


def gather(r, half):
    rows = slice(HALF * half, HALF * (half + 1))
    for b in range(STEPS):
        lanes = span(b)
        pick_ghost = (r.keys[rows, :] == pair_rows(r.source, b)).astype(BF16)
        r.from_ghost[b, rows, :] = pick_ghost
        found = dot(r.table[:, rows], pick_ghost)
        feats = r.near[:CH, lanes] + found[:CH]
        place = r.near[CH : CH + 8, lanes] + found[CH : CH + 8] + SIDE * found[CH + 8 : CH + 16]
        if half == NEAR:
            r.near[:CH, lanes] = feats
            r.near[CH : CH + 8, lanes] = place
        else:
            r.feats[:, lanes] = feats * SCALE
            r.geom[:, lanes] = place


def harmonics_of(x, y, z):
    return [
        ROOT3 * x * y,
        ROOT3 * y * z,
        0.5 * (2.0 * z * z - x * x - y * y),
        ROOT3 * x * z,
        0.5 * ROOT3 * (x * x - y * y),
    ]


def radial(r):
    v = r.geom[4:7, :]
    q = v[0:1] * v[0:1] + v[1:2] * v[1:2] + v[2:3] * v[2:3]
    keep = jnp.maximum(1.0 - q / CUT, 0.0)
    envelope = keep * keep
    d_envelope = keep * (-2.0 / CUT)
    centers = iota((NRB, NP), 0).astype(F32) * (CUT / (NRB - 1))
    away = q - centers
    bump = jnp.exp(-(away * away) / CUT)
    basis = bump * envelope
    d_basis = bump * (d_envelope - (2.0 / CUT) * away * envelope)
    z = dot(r.first_t[...], jnp.concatenate([stack_high_low(basis), stack_high_low(d_basis)], 1))
    h, slope = silu_parts(z[:, :NP])
    d = slope * z[:, NP:]
    z = dot(r.second_t[...], jnp.concatenate([stack_high_low(h), stack_high_low(d)], 1))
    h, slope = silu_parts(z[:, :NP])
    d = slope * z[:, NP:]
    r.hidden[0] = stack_high_low(h)
    r.hidden[1] = stack_high_low(d)


CHUNKS = ((0, 4), (4, 9))


def scatter(r):
    v = r.geom[4:7, :]
    ux, uy, uz = 0.5 * v[0:1], 0.5 * v[1:2], 0.5 * v[2:3]
    harmonics = [None, ux, uy, uz] + harmonics_of(ux, uy, uz)
    for first, last in CHUNKS:
        for b in range(STEPS):
            lanes = slice(BL * b, BL * (b + 1))
            for i in range(first, last):
                order = 0 if i == 0 else (1 if i < 4 else 2)
                part = slice(CH * order, CH * (order + 1))
                if i in (0, 1, 4):
                    z = dot(r.third_t[part, :], r.hidden[0, :, lanes])
                    r.radial[b, part, :] = z * r.feats[:, lanes]
                    z = dot(r.third_t[part, :], r.hidden[1, :, lanes])
                    r.slope[b, part, :] = z * r.feats[:, lanes]
                term = r.radial[b, part, :]
                if i:
                    term = term * harmonics[i][:, lanes]
                high, low = high_low(term)
                row = CH * i
                r.terms[row : row + CH, 512 * b : 512 * b + BL] = high.astype(BF16)
                r.terms[row : row + CH, 512 * b + BL : 512 * b + 512] = low.astype(BF16)
        rows = slice(CH * first, CH * last)
        r.moments[rows, :] = dot(r.terms[rows, :], r.by_pair[...])


def readout(r):
    def moment(i):
        return r.moments[CH * i : CH * (i + 1), :]

    squares = []
    for low, high in ((1, 4), (4, 9)):
        total = moment(low) * moment(low)
        for i in range(low + 1, high):
            total = total + moment(i) * moment(i)
        squares.append(total)
    invariants = jnp.concatenate([moment(0)] + squares, 0)
    high, low = high_low(invariants)
    mix_t = r.mix_t[...]
    mixed = dot(mix_t, high.astype(BF16)) + dot(mix_t, low.astype(BF16))
    head = r.head_t[...]
    h, slope = silu_parts(mixed)
    d_mixed = stack_high_low(head * slope)
    d_inv = dot(r.mix_two[...], d_mixed)
    for i in range(9):
        order = 0 if i == 0 else (1 if i < 4 else 2)
        grad = d_inv[CH * order : CH * (order + 1)]
        if order:
            grad = 2.0 * moment(i) * grad
        high, low = high_low(grad)
        r.grads[CH * i : CH * (i + 1), 0:AP] = high.astype(BF16)
        r.grads[CH * i : CH * (i + 1), AP : 2 * AP] = low.astype(BF16)
    r.out[0] = jnp.sum(head * h, axis=0, keepdims=True)[:, :A] + r.base[...]


def pulls(r):
    for b in range(STEPS):
        r.back[b] = dot(r.grads[...], r.to_own[b])
        v = r.geom[4:7, span(b)]
        along, across = [], []
        for i in range(9):
            order = 0 if i == 0 else (1 if i < 4 else 2)
            part = slice(CH * order, CH * (order + 1))
            grad = r.back[b, CH * i : CH * (i + 1), :]
            if order:
                along.append(jnp.sum(r.radial[b, part, :] * grad, axis=0, keepdims=True))
            slope = r.slope[b, part, :]
            across.append(jnp.sum(slope * grad, axis=0, keepdims=True))
        x, y, z = 0.5 * v[0:1], 0.5 * v[1:2], 0.5 * v[2:3]
        ax, ay, az, b0, b1, b2, b3, b4 = along
        dq = across[0] + x * across[1] + y * across[2] + z * across[3]
        for harmonic, c in zip(harmonics_of(x, y, z), across[4:]):
            dq = dq + harmonic * c
        gx = ax + ROOT3 * (y * b0 + z * b3 + x * b4) - x * b2
        gy = ay + ROOT3 * (x * b0 + z * b1 - y * b4) - y * b2
        gz = az + ROOT3 * (y * b1 + x * b3) + 2.0 * z * b2
        px = 0.5 * gx + 2.0 * dq * v[0:1]
        py = 0.5 * gy + 2.0 * dq * v[1:2]
        pz = 0.5 * gz + 2.0 * dq * v[2:3]
        pull = jnp.concatenate([px, py, pz, jnp.zeros((5, BL), F32)], 0)
        r.pull[b] = stack_high_low(pull)


def spread(pull_ref, pick):
    total = None
    for b in range(STEPS):
        part = dot(pull_ref[b], pick(b), NT)
        total = part if total is None else total + part
    return total[:8] + total[8:]


def give_ghosts(r, half):
    rows = slice(HALF * half, HALF * (half + 1))
    r.ghost[:, rows] = -spread(r.pull, lambda b: r.from_ghost[b, rows, :])


def own_forces(r):
    return spread(r.pull, lambda b: r.to_own[b, 0:AP, :] - r.from_own[b])


class Refs:
    def __init__(self, names, refs):
        for name, ref in zip(names, refs, strict=True):
            setattr(self, name, ref)


LOADS = {
    "pos": ((3, A), BF16),
    "feat": ((A, CH), BF16),
    "list": ((1, G), jnp.int32),
    "source": ((NB, 1, PB), jnp.int32),
    "target": ((NB, 1, PB), jnp.int32),
    "first": ((NRB, RH), BF16),
    "second": ((RH, RH), BF16),
    "third": ((RH, 3 * CH), BF16),
    "mix": ((3 * CH, CH), BF16),
    "head": ((1, CH), BF16),
    "species": ((1, A), jnp.int32),
    "count": ((1, 1, 1), jnp.int32),
    "shift": ((SPECIES,), F32),
}
EARLY = ("pos", "list", "feat")
WORK = {
    "first_t": ((RH, 2 * NRB), BF16),
    "second_t": ((RH, 2 * RH), BF16),
    "third_t": ((3 * CH, 2 * RH), BF16),
    "mix_t": ((CH, 3 * CH), BF16),
    "mix_two": ((3 * CH, 2 * CH), BF16),
    "head_t": ((CH, AP), F32),
    "base": ((1, A), F32),
    "upper": ((A, A), BF16),
    "own_table": ((CH + 16, AP), BF16),
    "table": ((CH + 16, GT), BF16),
    "keys": ((GT, BL), jnp.int32),
    "from_own": ((STEPS, AP, BL), BF16),
    "from_ghost": ((STEPS, GT, BL), BF16),
    "to_own": ((STEPS, 2 * AP, BL), BF16),
    "by_pair": ((STEPS * 2 * BL, AP), BF16),
    "near": ((CH + 8, NP), F32),
    "feats": ((CH, NP), F32),
    "geom": ((8, NP), F32),
    "hidden": ((2, 2 * RH, NP), BF16),
    "radial": ((STEPS, 3 * CH, BL), F32),
    "slope": ((STEPS, 3 * CH, BL), F32),
    "terms": ((9 * CH, STEPS * 2 * BL), BF16),
    "moments": ((9 * CH, AP), F32),
    "grads": ((9 * CH, 2 * AP), BF16),
    "back": ((STEPS, 9 * CH, BL), F32),
    "pull": ((STEPS, 16, BL), BF16),
    "ghost": ((8, GT), F32),
    "pick": ((GT, A), BF16),
    "sent": ((SENT, CH), BF16),
    "got": ((SENT, CH), BF16),
    "returned": ((26, 4, 128), F32),
}
INPUTS = ["hbm_" + name for name in LOADS]
NAMES = INPUTS + ["out"] + list(LOADS) + list(WORK)
NAMES += ["load_sem", "send_sem", "recv_sem", "back_send_sem", "back_recv_sem"]


def kernel(*refs):
    r = Refs(NAMES, refs)
    at = neighbours()
    loads = {}
    for i, name in enumerate(LOADS):
        loads[name] = pltpu.make_async_copy(
            getattr(r, "hbm_" + name), getattr(r, name), r.load_sem.at[i]
        )
        if name in EARLY:
            loads[name].start()
    barrier = enter(at)
    for name in LOADS:
        if name not in EARLY:
            loads[name].start()
    r.upper[...] = (iota((A, A), 0) <= iota((A, A), 1)).astype(BF16)
    for name in EARLY:
        loads.pop(name).wait()
    copies = {}

    def send(half):
        if half == FAR:
            pl.semaphore_wait(barrier, 26)
        for i, (slot, rows, row, lane) in ORDER:
            if lane // HALF != half:
                continue
            copies[i] = pltpu.make_async_remote_copy(
                src_ref=r.sent.at[row : row + rows, :],
                dst_ref=r.got.at[row : row + rows, :],
                send_sem=r.send_sem.at[i],
                recv_sem=r.recv_sem.at[i],
                device_id=at(slot, -1),
                device_id_type=MESH,
            )
            copies[i].start()

    choose(r.pos, r.feat, r.list, r.upper, r.pick, r.sent, send)
    for copy in loads.values():
        copy.wait()
    prepare(r)
    for half in (NEAR, FAR):
        for members in tiles_of(half).values():
            for i, _ in members:
                copies[i].wait_recv()
        ghost_table(r.got, r.table, r.keys, half)
        gather(r, half)
    radial(r)
    scatter(r)
    readout(r)
    pulls(r)
    returns = {}
    for half in (FAR, NEAR):
        give_ghosts(r, half)
        for i, (slot, rows, _, lane) in ORDER:
            if lane // HALF != half:
                continue
            start = lane // 128 * 128
            returns[i] = pltpu.make_async_remote_copy(
                src_ref=r.ghost.at[0:4, start : start + 128],
                dst_ref=r.returned.at[i],
                send_sem=r.back_send_sem.at[i],
                recv_sem=r.back_recv_sem.at[i],
                device_id=at(slot, 1),
                device_id_type=MESH,
            )
            returns[i].start()
    total = own_forces(r)[:4, :A]
    for copy in copies.values():
        copy.wait_send()
    for half in (NEAR, FAR):
        tiles = []
        for members in tiles_of(half).values():
            for i, _ in members:
                returns[i].wait_recv()
            got = [r.returned[i] for i, _ in members]
            tiles.append(group_lanes(got, 128 // len(members)))
        got = stack_high_low(jnp.concatenate(tiles, 1))
        sums = dot(got, r.pick[HALF * half : HALF * (half + 1), :])
        total = total + sums[:4] + sums[4:]
    for axis in range(3):
        r.out[axis + 1] = total[axis : axis + 1]
    for copy in returns.values():
        copy.wait_send()


def split_kernel(both_ref, energy_ref, force_ref, sem):
    first = pltpu.make_async_copy(both_ref.at[0:1], energy_ref, sem.at[0])
    second = pltpu.make_async_copy(both_ref.at[1:4], force_ref, sem.at[1])
    first.start()
    second.start()
    first.wait()
    second.wait()


def vmem():
    return pl.BlockSpec(memory_space=pltpu.VMEM)


def shape(dims, kind=F32):
    return jax.ShapeDtypeStruct(dims, kind)


def shards(
    positions,
    features,
    species,
    species_shift,
    send_index,
    pair_target,
    pair_source,
    block_count,
    radial_first,
    radial_second,
    radial_third,
    invariant_mix,
    energy_head,
):
    both = pl.pallas_call(
        kernel,
        out_shape=pltpu.VMEM((4, 1, A), F32),
        in_specs=[pl.BlockSpec(memory_space=pl.ANY)] * len(LOADS),
        out_specs=vmem(),
        scratch_shapes=[
            (pltpu.SMEM if name in ("count", "shift") else pltpu.VMEM)(*spec)
            for name, spec in LOADS.items()
        ]
        + [pltpu.VMEM(*spec) for spec in WORK.values()]
        + [pltpu.SemaphoreType.DMA((len(LOADS),))]
        + [pltpu.SemaphoreType.DMA((26,))] * 4,
        compiler_params=pltpu.CompilerParams(
            collective_id=0, has_side_effects=True, vmem_limit_bytes=56 * 2**20
        ),
        name="layer",
    )(
        positions.reshape(3, A),
        jnp.swapaxes(features, 3, 4).reshape(A, CH),
        send_index.reshape(1, G),
        pair_source.reshape(NB, 1, PB),
        pair_target.reshape(NB, 1, PB),
        radial_first,
        radial_second,
        radial_third,
        invariant_mix,
        energy_head.reshape(1, CH),
        species.reshape(1, A),
        block_count,
        species_shift,
    )
    energies, forces = pl.pallas_call(
        split_kernel,
        out_shape=(shape((1, 1, A)), shape((3, 1, A))),
        in_specs=[vmem()],
        out_specs=(pl.BlockSpec(memory_space=pl.ANY),) * 2,
        scratch_shapes=[pltpu.SemaphoreType.DMA((2,))],
        compiler_params=pltpu.CompilerParams(vmem_limit_bytes=2**20),
        name="split",
    )(both)
    return (energies.reshape(1, 1, 1, A), forces.reshape(1, 1, 1, 3, A))


def solution(mesh):
    split = ("gx", "gy", "gz")
    return jax.shard_map(
        shards,
        mesh=mesh,
        in_specs=(
            P(*split, None, None),
            P(*split, None, None),
            P(*split, None),
            P(),
            P(*split, None),
            P(*split, None, None),
            P(*split, None, None),
            P(*split),
            P(),
            P(),
            P(),
            P(),
            P(),
        ),
        out_specs=(P(*split, None), P(*split, None, None)),
        check_vma=False,
    )
```

```python
import functools

import jax
import jax.numpy as jnp
import numpy as np
from jax import lax
from jax.experimental import pallas as pl
from jax.experimental.pallas import tpu as pltpu
from jax.sharding import PartitionSpec as P

A = 432
AP = 512
G = 304
CH = 128
NB = 10
PB = 128
BL = 256
STEPS = NB * PB // BL
NP = NB * PB
RH = 64
NRB = 8
SPECIES = 10
GT = 1280
SENT = 1088
CELL = 2.5
SIDE = 15.0
CUT = 25.0
MID = 152.0
SCALE = 0.15
ROOT3 = 1.7320508075688772

F32 = jnp.float32
BF16 = jnp.bfloat16
MESH = pl.DeviceIdType.MESH
NN = (((1,), (0,)), ((), ()))
NT = (((1,), (1,)), ((), ()))


def offset_of(slot):
    return (slot // 9 - 1, slot // 3 % 3 - 1, slot % 3 - 1)


def places():
    out = []
    row, lane = 0, 0
    for far in (False, True):
        for kind, rows, lanes in ((1, 96, 128), (2, 32, 32), (3, 16, 16)):
            for slot in range(27):
                offset = offset_of(slot)
                if sum(abs(c) for c in offset) == kind and (offset[2] != 0) == far:
                    out.append((slot, rows, row, lane))
                    row, lane = row + rows, lane + lanes
    return out


PLACES = places()
HALF = GT // 2
NEAR, FAR = 0, 1


def tiles_of(half):
    tiles = {}
    for i, place in enumerate(PLACES):
        if place[3] // HALF == half:
            tiles.setdefault(place[3] // 128, []).append((i, place))
    return tiles


def far_first():
    def way(place):
        x, y, z = offset_of(place[0])
        return -(4 * abs(z) + 2 * abs(y) + abs(x))

    return sorted(enumerate(PLACES), key=lambda item: way(item[1]))


ORDER = far_first()


def dot(a, b, dims=NN):
    return lax.dot_general(a, b, dims, preferred_element_type=F32)


def iota(shape, dim):
    return lax.broadcasted_iota(jnp.int32, shape, dim)


def high_low(x):
    high = x.astype(BF16).astype(F32)
    return high, x - high


def neighbours():
    steps = {}
    for axis, size in (("gx", 4), ("gy", 4), ("gz", 16)):
        me = lax.axis_index(axis)
        steps[axis] = {0: me, 1: lax.rem(me + 1, size), -1: lax.rem(me + size - 1, size)}

    def at(slot, sign):
        offset = offset_of(slot)
        return tuple(steps[axis][sign * o] for axis, o in zip(("gx", "gy", "gz"), offset))

    return at


def enter(at):
    barrier = pltpu.get_barrier_semaphore()
    for _, (slot, *_) in ORDER:
        pl.semaphore_signal(barrier, inc=1, device_id=at(slot, 1), device_id_type=MESH)
    return barrier


def choose(pos_ref, feat_ref, list_ref, upper_ref, pick_ref, send_ref, send):
    pos = pos_ref[...].astype(F32)
    entry = (iota((A, G), 0) == list_ref[...]).astype(BF16)
    ids = iota((8, G), 1).astype(F32)
    coded = jnp.where(ids < MID, ids - MID, ids - (MID - 1.0))
    code = dot(coded.astype(BF16), entry, NT)
    member = (code[0:1] != 0.0).astype(F32)
    slots = iota((32, A), 0)
    ix = (slots >= 9).astype(jnp.int32) + (slots >= 18).astype(jnp.int32)
    rest = slots - 9 * ix
    iy = (rest >= 3).astype(jnp.int32) + (rest >= 6).astype(jnp.int32)
    iz = rest - 3 * iy
    strict = member
    closed = member
    for axis, index in enumerate((ix, iy, iz)):
        x = pos[axis : axis + 1]
        one = jnp.ones((1, A), F32)
        strict = strict * jnp.where(
            index == 0,
            (x > SIDE - CELL).astype(F32),
            jnp.where(index == 2, (x < CELL).astype(F32), one),
        )
        closed = closed * jnp.where(
            index == 0,
            (x >= SIDE - CELL).astype(F32),
            jnp.where(index == 2, (x <= CELL).astype(F32), one),
        )
    both = jnp.concatenate([strict, closed - strict], 0)
    count = dot(both.astype(BF16), upper_ref[...])
    total = count[:32, A - 1 : A]
    rank = jnp.where(
        strict > 0.0,
        count[:32] - 1.0,
        jnp.where(closed > 0.0, total + count[32:] - 1.0, -1.0),
    )
    meta = jnp.concatenate([jnp.zeros((4, A), F32), pos, code[0:1]], 0).astype(BF16)
    feat = feat_ref[...]
    for half in (FAR, NEAR):
        for t, members in tiles_of(half).items():
            tile = slice(128 * t, 128 * (t + 1))
            rows = members[0][1][1]
            for _, (slot, _, _, lane) in members:
                tall = 128 if rows == 96 else rows
                step = iota((tall, A), 0)
                step = jnp.where(step < rows - 4, step, -2).astype(F32)
                pick_ref[lane : lane + tall, :] = (step == rank[slot : slot + 1]).astype(BF16)
            block = dot(pick_ref[tile, :], feat)
            told = dot(meta, pick_ref[tile, :], NT)
            pieces = []
            for i in range(len(members)):
                pieces.append(block[rows * i : rows * i + rows - 8])
                pieces.append(block[rows * i + rows - 8 : rows * (i + 1)] + told)
            row = members[0][1][2]
            send_ref[row : row + rows * len(members), :] = jnp.concatenate(pieces, 0).astype(BF16)
        send(half)


def group_lanes(tiles, width):
    lane = iota(tiles[0].shape, 1)
    out = tiles[0]
    for i in range(1, len(tiles)):
        out = jnp.where(lane >= width * i, tiles[i], out)
    return out


def ghost_table(got_ref, table_ref, key_ref, half):
    for t, members in tiles_of(half).items():
        members = [place for _, place in members]
        width = 128 // len(members)
        row, rows = members[0][2], members[0][1]
        if rows == 96:
            feats = jnp.concatenate(
                [got_ref[row : row + 96, :].astype(F32), jnp.zeros((32, CH), F32)], 0
            )
        else:
            feats = got_ref[row : row + 128, :].astype(F32)
        table_ref[0:CH, 128 * t : 128 * (t + 1)] = feats.T.astype(BF16)
        told, offs = [], []
        for slot, rows, row, _ in members:
            told.append(got_ref[row + rows - 16 : row + rows, :].astype(F32)[8:16])
        told = group_lanes(told, width)
        sub = iota((8, 128), 0)
        for slot, *_ in members:
            o = offset_of(slot)
            offs.append(
                jnp.where(
                    sub == 4,
                    float(o[0]),
                    jnp.where(sub == 5, float(o[1]), jnp.where(sub == 6, float(o[2]), 0.0)),
                )
            )
        offs = group_lanes(offs, width)
        base = group_lanes(
            [jnp.full((8, 128), float(A + G * slot), F32) for slot, *_ in members], width
        )
        table_ref[CH : CH + 16, 128 * t : 128 * (t + 1)] = jnp.concatenate(
            [told, offs], 0
        ).astype(BF16)
        code = told[7:8]
        index = jnp.where(code < 0.0, code + MID, code + (MID - 1.0)) + base[0:1]
        key = jnp.where(code == 0.0, -5.0, index)
        column = jnp.broadcast_to(key, (128, 128)).T.astype(jnp.int32)
        key_ref[128 * t : 128 * (t + 1), :] = jnp.concatenate([column, column], 1)


def silu_parts(z):
    s = 0.5 * jnp.tanh(0.5 * z) + 0.5
    h = z * s
    return h, s + h * (1.0 - s)


def stack_high_low(x):
    return jnp.concatenate(high_low(x), 0).astype(BF16)


def span(b):
    return slice(BL * b, BL * (b + 1))


def pair_rows(ref, b):
    return jnp.concatenate([ref[2 * b], ref[2 * b + 1]], 1)


def twice_across(ref):
    x = ref[...].astype(F32).T
    return jnp.concatenate([x, x], 1).astype(BF16)


def prepare(r):
    r.own_table[...] = jnp.zeros_like(r.own_table)
    feat = r.feat[...].astype(F32).T
    r.own_table[0:CH, 0:A] = feat.astype(BF16)
    none = jnp.zeros((4, A), F32)
    pos = jnp.concatenate([none, r.pos[...].astype(F32), none, none, none[:1]], 0)
    r.own_table[CH : CH + 16, 0:A] = pos.astype(BF16)
    r.first_t[...] = twice_across(r.first)
    r.second_t[...] = twice_across(r.second)
    r.third_t[...] = twice_across(r.third)
    mix = r.mix[...]
    r.mix_t[...] = mix.astype(F32).T.astype(BF16)
    r.mix_two[...] = jnp.concatenate([mix, mix], 1)
    head = jnp.broadcast_to(r.head[...].astype(F32), (128, 128)).T
    r.head_t[...] = jnp.concatenate([head] * 4, 1)
    kinds = r.species[...]
    base = jnp.zeros((1, A), F32)
    for k in range(SPECIES):
        base = base + jnp.where(kinds == k, r.shift[k], 0.0)
    r.base[...] = base
    count = r.count[0, 0, 0]

    for b in range(STEPS):
        source = pair_rows(r.source, b)
        target = pair_rows(r.target, b)
        live = 2 * b + (iota((1, BL), 1) >= PB).astype(jnp.int32) < count
        target = jnp.where(live, target, -1)
        atoms = iota((AP, BL), 0)
        pick_own = (atoms == source).astype(BF16)
        pick_target = (atoms == target).astype(BF16)
        r.from_own[b] = pick_own
        r.to_own[b, 0:AP, :] = pick_target
        r.to_own[b, AP : 2 * AP, :] = pick_target
        across = iota((PB, AP), 1)
        for half in range(2):
            part = jnp.broadcast_to(target[:, PB * half : PB * (half + 1)], (PB, PB))
            column = part.astype(F32).T.astype(jnp.int32)
            pick = (across == jnp.concatenate([column] * 4, 1)).astype(BF16)
            r.by_pair[512 * b + PB * half : 512 * b + PB * (half + 1), :] = pick
            r.by_pair[512 * b + BL + PB * half : 512 * b + BL + PB * (half + 1), :] = pick
        near = dot(r.own_table[...], pick_own)
        here = dot(r.own_table[CH : CH + 16, :], pick_target)
        r.near[:, span(b)] = jnp.concatenate([near[:CH], near[CH : CH + 8] - here[:8]], 0)


def gather(r, half):
    rows = slice(HALF * half, HALF * (half + 1))
    for b in range(STEPS):
        lanes = span(b)
        pick_ghost = (r.keys[rows, :] == pair_rows(r.source, b)).astype(BF16)
        r.from_ghost[b, rows, :] = pick_ghost
        found = dot(r.table[:, rows], pick_ghost)
        feats = r.near[:CH, lanes] + found[:CH]
        place = r.near[CH : CH + 8, lanes] + found[CH : CH + 8] + SIDE * found[CH + 8 : CH + 16]
        if half == NEAR:
            r.near[:CH, lanes] = feats
            r.near[CH : CH + 8, lanes] = place
        else:
            r.feats[:, lanes] = feats * SCALE
            r.geom[:, lanes] = place


def harmonics_of(x, y, z):
    return [
        ROOT3 * x * y,
        ROOT3 * y * z,
        0.5 * (2.0 * z * z - x * x - y * y),
        ROOT3 * x * z,
        0.5 * ROOT3 * (x * x - y * y),
    ]


def radial(r):
    v = r.geom[4:7, :]
    q = v[0:1] * v[0:1] + v[1:2] * v[1:2] + v[2:3] * v[2:3]
    keep = jnp.maximum(1.0 - q / CUT, 0.0)
    envelope = keep * keep
    d_envelope = keep * (-2.0 / CUT)
    centers = iota((NRB, NP), 0).astype(F32) * (CUT / (NRB - 1))
    away = q - centers
    bump = jnp.exp(-(away * away) / CUT)
    basis = bump * envelope
    d_basis = bump * (d_envelope - (2.0 / CUT) * away * envelope)
    z = dot(r.first_t[...], jnp.concatenate([stack_high_low(basis), stack_high_low(d_basis)], 1))
    h, slope = silu_parts(z[:, :NP])
    d = slope * z[:, NP:]
    z = dot(r.second_t[...], jnp.concatenate([stack_high_low(h), stack_high_low(d)], 1))
    h, slope = silu_parts(z[:, :NP])
    d = slope * z[:, NP:]
    r.hidden[0] = stack_high_low(h)
    r.hidden[1] = stack_high_low(d)


CHUNKS = ((0, 4), (4, 9))


def scatter(r):
    v = r.geom[4:7, :]
    ux, uy, uz = 0.5 * v[0:1], 0.5 * v[1:2], 0.5 * v[2:3]
    harmonics = [None, ux, uy, uz] + harmonics_of(ux, uy, uz)
    for first, last in CHUNKS:
        for b in range(STEPS):
            lanes = slice(BL * b, BL * (b + 1))
            for i in range(first, last):
                order = 0 if i == 0 else (1 if i < 4 else 2)
                part = slice(CH * order, CH * (order + 1))
                if i in (0, 1, 4):
                    z = dot(r.third_t[part, :], r.hidden[0, :, lanes])
                    r.radial[b, part, :] = z * r.feats[:, lanes]
                term = r.radial[b, part, :]
                if i:
                    term = term * harmonics[i][:, lanes]
                high, low = high_low(term)
                row = CH * i
                r.terms[row : row + CH, 512 * b : 512 * b + BL] = high.astype(BF16)
                r.terms[row : row + CH, 512 * b + BL : 512 * b + 512] = low.astype(BF16)
        rows = slice(CH * first, CH * last)
        r.moments[rows, :] = dot(r.terms[rows, :], r.by_pair[...])


def readout(r):
    def moment(i):
        return r.moments[CH * i : CH * (i + 1), :]

    squares = []
    for low, high in ((1, 4), (4, 9)):
        total = moment(low) * moment(low)
        for i in range(low + 1, high):
            total = total + moment(i) * moment(i)
        squares.append(total)
    invariants = jnp.concatenate([moment(0)] + squares, 0)
    high, low = high_low(invariants)
    mix_t = r.mix_t[...]
    mixed = dot(mix_t, high.astype(BF16)) + dot(mix_t, low.astype(BF16))
    head = r.head_t[...]
    h, slope = silu_parts(mixed)
    d_mixed = stack_high_low(head * slope)
    d_inv = dot(r.mix_two[...], d_mixed)
    for i in range(9):
        order = 0 if i == 0 else (1 if i < 4 else 2)
        grad = d_inv[CH * order : CH * (order + 1)]
        if order:
            grad = 2.0 * moment(i) * grad
        high, low = high_low(grad)
        r.grads[CH * i : CH * (i + 1), 0:AP] = high.astype(BF16)
        r.grads[CH * i : CH * (i + 1), AP : 2 * AP] = low.astype(BF16)
    r.out[0] = jnp.sum(head * h, axis=0, keepdims=True)[:, :A] + r.base[...]


def pulls(r):
    for b in range(STEPS):
        d = dot(r.third_t[...], r.hidden[1, :, span(b)])
        r.back[b] = dot(r.grads[...], r.to_own[b])
        v = r.geom[4:7, span(b)]
        along, across = [], []
        for i in range(9):
            order = 0 if i == 0 else (1 if i < 4 else 2)
            part = slice(CH * order, CH * (order + 1))
            grad = r.back[b, CH * i : CH * (i + 1), :]
            if order:
                along.append(jnp.sum(r.radial[b, part, :] * grad, axis=0, keepdims=True))
            slope = d[part] * r.feats[:, span(b)]
            across.append(jnp.sum(slope * grad, axis=0, keepdims=True))
        x, y, z = 0.5 * v[0:1], 0.5 * v[1:2], 0.5 * v[2:3]
        ax, ay, az, b0, b1, b2, b3, b4 = along
        dq = across[0] + x * across[1] + y * across[2] + z * across[3]
        for harmonic, c in zip(harmonics_of(x, y, z), across[4:]):
            dq = dq + harmonic * c
        gx = ax + ROOT3 * (y * b0 + z * b3 + x * b4) - x * b2
        gy = ay + ROOT3 * (x * b0 + z * b1 - y * b4) - y * b2
        gz = az + ROOT3 * (y * b1 + x * b3) + 2.0 * z * b2
        px = 0.5 * gx + 2.0 * dq * v[0:1]
        py = 0.5 * gy + 2.0 * dq * v[1:2]
        pz = 0.5 * gz + 2.0 * dq * v[2:3]
        pull = jnp.concatenate([px, py, pz, jnp.zeros((5, BL), F32)], 0)
        r.pull[b] = stack_high_low(pull)


def spread(pull_ref, pick):
    total = None
    for b in range(STEPS):
        part = dot(pull_ref[b], pick(b), NT)
        total = part if total is None else total + part
    return total[:8] + total[8:]


def give_ghosts(r, half):
    rows = slice(HALF * half, HALF * (half + 1))
    r.ghost[:, rows] = -spread(r.pull, lambda b: r.from_ghost[b, rows, :])


def own_forces(r):
    return spread(r.pull, lambda b: r.to_own[b, 0:AP, :] - r.from_own[b])


class Refs:
    def __init__(self, names, refs):
        for name, ref in zip(names, refs, strict=True):
            setattr(self, name, ref)


LOADS = {
    "pos": ((3, A), BF16),
    "feat": ((A, CH), BF16),
    "list": ((1, G), jnp.int32),
    "source": ((NB, 1, PB), jnp.int32),
    "target": ((NB, 1, PB), jnp.int32),
    "first": ((NRB, RH), BF16),
    "second": ((RH, RH), BF16),
    "third": ((RH, 3 * CH), BF16),
    "mix": ((3 * CH, CH), BF16),
    "head": ((1, CH), BF16),
    "species": ((1, A), jnp.int32),
    "count": ((1, 1, 1), jnp.int32),
    "shift": ((SPECIES,), F32),
}
EARLY = ("pos", "list", "feat")
WORK = {
    "first_t": ((RH, 2 * NRB), BF16),
    "second_t": ((RH, 2 * RH), BF16),
    "third_t": ((3 * CH, 2 * RH), BF16),
    "mix_t": ((CH, 3 * CH), BF16),
    "mix_two": ((3 * CH, 2 * CH), BF16),
    "head_t": ((CH, AP), F32),
    "base": ((1, A), F32),
    "upper": ((A, A), BF16),
    "own_table": ((CH + 16, AP), BF16),
    "table": ((CH + 16, GT), BF16),
    "keys": ((GT, BL), jnp.int32),
    "from_own": ((STEPS, AP, BL), BF16),
    "from_ghost": ((STEPS, GT, BL), BF16),
    "to_own": ((STEPS, 2 * AP, BL), BF16),
    "by_pair": ((STEPS * 2 * BL, AP), BF16),
    "near": ((CH + 8, NP), F32),
    "feats": ((CH, NP), F32),
    "geom": ((8, NP), F32),
    "hidden": ((2, 2 * RH, NP), BF16),
    "radial": ((STEPS, 3 * CH, BL), F32),
    "terms": ((9 * CH, STEPS * 2 * BL), BF16),
    "moments": ((9 * CH, AP), F32),
    "grads": ((9 * CH, 2 * AP), BF16),
    "back": ((STEPS, 9 * CH, BL), F32),
    "pull": ((STEPS, 16, BL), BF16),
    "ghost": ((8, GT), F32),
    "pick": ((GT, A), BF16),
    "sent": ((SENT, CH), BF16),
    "got": ((SENT, CH), BF16),
    "returned": ((26, 4, 128), F32),
}
INPUTS = ["hbm_" + name for name in LOADS]
NAMES = INPUTS + ["out"] + list(LOADS) + list(WORK)
NAMES += ["load_sem", "send_sem", "recv_sem", "back_send_sem", "back_recv_sem"]


def kernel(*refs):
    r = Refs(NAMES, refs)
    at = neighbours()
    loads = {}
    for i, name in enumerate(LOADS):
        loads[name] = pltpu.make_async_copy(
            getattr(r, "hbm_" + name), getattr(r, name), r.load_sem.at[i]
        )
        if name in EARLY:
            loads[name].start()
    barrier = enter(at)
    for name in LOADS:
        if name not in EARLY:
            loads[name].start()
    r.upper[...] = (iota((A, A), 0) <= iota((A, A), 1)).astype(BF16)
    for name in EARLY:
        loads.pop(name).wait()
    copies = {}

    def send(half):
        if half == FAR:
            pl.semaphore_wait(barrier, 26)
        for i, (slot, rows, row, lane) in ORDER:
            if lane // HALF != half:
                continue
            copies[i] = pltpu.make_async_remote_copy(
                src_ref=r.sent.at[row : row + rows, :],
                dst_ref=r.got.at[row : row + rows, :],
                send_sem=r.send_sem.at[i],
                recv_sem=r.recv_sem.at[i],
                device_id=at(slot, -1),
                device_id_type=MESH,
            )
            copies[i].start()

    choose(r.pos, r.feat, r.list, r.upper, r.pick, r.sent, send)
    for copy in loads.values():
        copy.wait()
    prepare(r)
    for half in (NEAR, FAR):
        for members in tiles_of(half).values():
            for i, _ in members:
                copies[i].wait_recv()
        ghost_table(r.got, r.table, r.keys, half)
        gather(r, half)
    radial(r)
    scatter(r)
    readout(r)
    pulls(r)
    returns = {}
    for half in (FAR, NEAR):
        give_ghosts(r, half)
        for i, (slot, rows, _, lane) in ORDER:
            if lane // HALF != half:
                continue
            start = lane // 128 * 128
            returns[i] = pltpu.make_async_remote_copy(
                src_ref=r.ghost.at[0:4, start : start + 128],
                dst_ref=r.returned.at[i],
                send_sem=r.back_send_sem.at[i],
                recv_sem=r.back_recv_sem.at[i],
                device_id=at(slot, 1),
                device_id_type=MESH,
            )
            returns[i].start()
    total = own_forces(r)[:4, :A]
    for copy in copies.values():
        copy.wait_send()
    for half in (NEAR, FAR):
        tiles = []
        for members in tiles_of(half).values():
            for i, _ in members:
                returns[i].wait_recv()
            got = [r.returned[i] for i, _ in members]
            tiles.append(group_lanes(got, 128 // len(members)))
        got = stack_high_low(jnp.concatenate(tiles, 1))
        sums = dot(got, r.pick[HALF * half : HALF * (half + 1), :])
        total = total + sums[:4] + sums[4:]
    for axis in range(3):
        r.out[axis + 1] = total[axis : axis + 1]
    for copy in returns.values():
        copy.wait_send()


def split_kernel(both_ref, energy_ref, force_ref, sem):
    first = pltpu.make_async_copy(both_ref.at[0:1], energy_ref, sem.at[0])
    second = pltpu.make_async_copy(both_ref.at[1:4], force_ref, sem.at[1])
    first.start()
    second.start()
    first.wait()
    second.wait()


def vmem():
    return pl.BlockSpec(memory_space=pltpu.VMEM)


def shape(dims, kind=F32):
    return jax.ShapeDtypeStruct(dims, kind)


def shards(
    positions,
    features,
    species,
    species_shift,
    send_index,
    pair_target,
    pair_source,
    block_count,
    radial_first,
    radial_second,
    radial_third,
    invariant_mix,
    energy_head,
):
    both = pl.pallas_call(
        kernel,
        out_shape=pltpu.VMEM((4, 1, A), F32),
        in_specs=[pl.BlockSpec(memory_space=pl.ANY)] * len(LOADS),
        out_specs=vmem(),
        scratch_shapes=[
            (pltpu.SMEM if name in ("count", "shift") else pltpu.VMEM)(*spec)
            for name, spec in LOADS.items()
        ]
        + [pltpu.VMEM(*spec) for spec in WORK.values()]
        + [pltpu.SemaphoreType.DMA((len(LOADS),))]
        + [pltpu.SemaphoreType.DMA((26,))] * 4,
        compiler_params=pltpu.CompilerParams(
            collective_id=0, has_side_effects=True, vmem_limit_bytes=56 * 2**20
        ),
        name="layer",
    )(
        positions.reshape(3, A),
        jnp.swapaxes(features, 3, 4).reshape(A, CH),
        send_index.reshape(1, G),
        pair_source.reshape(NB, 1, PB),
        pair_target.reshape(NB, 1, PB),
        radial_first,
        radial_second,
        radial_third,
        invariant_mix,
        energy_head.reshape(1, CH),
        species.reshape(1, A),
        block_count,
        species_shift,
    )
    energies, forces = pl.pallas_call(
        split_kernel,
        out_shape=(shape((1, 1, A)), shape((3, 1, A))),
        in_specs=[vmem()],
        out_specs=(pl.BlockSpec(memory_space=pl.ANY),) * 2,
        scratch_shapes=[pltpu.SemaphoreType.DMA((2,))],
        compiler_params=pltpu.CompilerParams(vmem_limit_bytes=2**20),
        name="split",
    )(both)
    return (energies.reshape(1, 1, 1, A), forces.reshape(1, 1, 1, 3, A))


def solution(mesh):
    split = ("gx", "gy", "gz")
    return jax.shard_map(
        shards,
        mesh=mesh,
        in_specs=(
            P(*split, None, None),
            P(*split, None, None),
            P(*split, None),
            P(),
            P(*split, None),
            P(*split, None, None),
            P(*split, None, None),
            P(*split),
            P(),
            P(),
            P(),
            P(),
            P(),
        ),
        out_specs=(P(*split, None), P(*split, None, None)),
        check_vma=False,
    )
```

```python
import functools

import jax
import jax.numpy as jnp
import numpy as np
from jax import lax
from jax.experimental import pallas as pl
from jax.experimental.pallas import tpu as pltpu
from jax.sharding import PartitionSpec as P

A = 432
AP = 512
G = 304
CH = 128
NB = 10
PB = 128
BL = 256
STEPS = NB * PB // BL
NP = NB * PB
RH = 64
NRB = 8
SPECIES = 10
GT = 1280
SENT = 1088
CELL = 2.5
SIDE = 15.0
CUT = 25.0
MID = 152.0
SCALE = 0.15
ROOT3 = 1.7320508075688772

F32 = jnp.float32
BF16 = jnp.bfloat16
MESH = pl.DeviceIdType.MESH
NN = (((1,), (0,)), ((), ()))
NT = (((1,), (1,)), ((), ()))


def offset_of(slot):
    return (slot // 9 - 1, slot // 3 % 3 - 1, slot % 3 - 1)


def places():
    out = []
    row, lane = 0, 0
    for far in (False, True):
        for kind, rows, lanes in ((1, 96, 128), (2, 32, 32), (3, 16, 16)):
            for slot in range(27):
                offset = offset_of(slot)
                if sum(abs(c) for c in offset) == kind and (offset[2] != 0) == far:
                    out.append((slot, rows, row, lane))
                    row, lane = row + rows, lane + lanes
    return out


PLACES = places()
HALF = GT // 2
NEAR, FAR = 0, 1


def tiles_of(half):
    tiles = {}
    for i, place in enumerate(PLACES):
        if place[3] // HALF == half:
            tiles.setdefault(place[3] // 128, []).append((i, place))
    return tiles


def far_first():
    def way(place):
        x, y, z = offset_of(place[0])
        return -(4 * abs(z) + 2 * abs(y) + abs(x))

    return sorted(enumerate(PLACES), key=lambda item: way(item[1]))


ORDER = far_first()


def dot(a, b, dims=NN):
    return lax.dot_general(a, b, dims, preferred_element_type=F32)


def iota(shape, dim):
    return lax.broadcasted_iota(jnp.int32, shape, dim)


def high_low(x):
    high = x.astype(BF16).astype(F32)
    return high, x - high


def neighbours():
    steps = {}
    for axis, size in (("gx", 4), ("gy", 4), ("gz", 16)):
        me = lax.axis_index(axis)
        steps[axis] = {0: me, 1: lax.rem(me + 1, size), -1: lax.rem(me + size - 1, size)}

    def at(slot, sign):
        offset = offset_of(slot)
        return tuple(steps[axis][sign * o] for axis, o in zip(("gx", "gy", "gz"), offset))

    return at


def enter(at):
    barrier = pltpu.get_barrier_semaphore()
    for _, (slot, *_) in ORDER:
        pl.semaphore_signal(barrier, inc=1, device_id=at(slot, 1), device_id_type=MESH)
    return barrier


def choose(pos_ref, feat_ref, list_ref, upper_ref, pick_ref, send_ref, send):
    pos = pos_ref[...].astype(F32)
    entry = (iota((A, G), 0) == list_ref[...]).astype(BF16)
    ids = iota((8, G), 1).astype(F32)
    coded = jnp.where(ids < MID, ids - MID, ids - (MID - 1.0))
    code = dot(coded.astype(BF16), entry, NT)
    member = (code[0:1] != 0.0).astype(F32)
    slots = iota((32, A), 0)
    ix = (slots >= 9).astype(jnp.int32) + (slots >= 18).astype(jnp.int32)
    rest = slots - 9 * ix
    iy = (rest >= 3).astype(jnp.int32) + (rest >= 6).astype(jnp.int32)
    iz = rest - 3 * iy
    strict = member
    closed = member
    for axis, index in enumerate((ix, iy, iz)):
        x = pos[axis : axis + 1]
        one = jnp.ones((1, A), F32)
        strict = strict * jnp.where(
            index == 0,
            (x > SIDE - CELL).astype(F32),
            jnp.where(index == 2, (x < CELL).astype(F32), one),
        )
        closed = closed * jnp.where(
            index == 0,
            (x >= SIDE - CELL).astype(F32),
            jnp.where(index == 2, (x <= CELL).astype(F32), one),
        )
    both = jnp.concatenate([strict, closed - strict], 0)
    count = dot(both.astype(BF16), upper_ref[...])
    total = count[:32, A - 1 : A]
    rank = jnp.where(
        strict > 0.0,
        count[:32] - 1.0,
        jnp.where(closed > 0.0, total + count[32:] - 1.0, -1.0),
    )
    meta = jnp.concatenate([jnp.zeros((4, A), F32), pos, code[0:1]], 0).astype(BF16)
    feat = feat_ref[...]
    for half in (FAR, NEAR):
        for t, members in tiles_of(half).items():
            tile = slice(128 * t, 128 * (t + 1))
            rows = members[0][1][1]
            for _, (slot, _, _, lane) in members:
                tall = 128 if rows == 96 else rows
                step = iota((tall, A), 0)
                step = jnp.where(step < rows - 4, step, -2).astype(F32)
                pick_ref[lane : lane + tall, :] = (step == rank[slot : slot + 1]).astype(BF16)
            block = dot(pick_ref[tile, :], feat)
            told = dot(meta, pick_ref[tile, :], NT)
            pieces = []
            for i in range(len(members)):
                pieces.append(block[rows * i : rows * i + rows - 8])
                pieces.append(block[rows * i + rows - 8 : rows * (i + 1)] + told)
            row = members[0][1][2]
            send_ref[row : row + rows * len(members), :] = jnp.concatenate(pieces, 0).astype(BF16)
        send(half)


def group_lanes(tiles, width):
    lane = iota(tiles[0].shape, 1)
    out = tiles[0]
    for i in range(1, len(tiles)):
        out = jnp.where(lane >= width * i, tiles[i], out)
    return out


def ghost_table(got_ref, table_ref, key_ref, half):
    for t, members in tiles_of(half).items():
        members = [place for _, place in members]
        width = 128 // len(members)
        row, rows = members[0][2], members[0][1]
        if rows == 96:
            feats = jnp.concatenate(
                [got_ref[row : row + 96, :].astype(F32), jnp.zeros((32, CH), F32)], 0
            )
        else:
            feats = got_ref[row : row + 128, :].astype(F32)
        table_ref[0:CH, 128 * t : 128 * (t + 1)] = feats.T.astype(BF16)
        told, offs = [], []
        for slot, rows, row, _ in members:
            told.append(got_ref[row + rows - 16 : row + rows, :].astype(F32)[8:16])
        told = group_lanes(told, width)
        sub = iota((8, 128), 0)
        for slot, *_ in members:
            o = offset_of(slot)
            offs.append(
                jnp.where(
                    sub == 4,
                    float(o[0]),
                    jnp.where(sub == 5, float(o[1]), jnp.where(sub == 6, float(o[2]), 0.0)),
                )
            )
        offs = group_lanes(offs, width)
        base = group_lanes(
            [jnp.full((8, 128), float(A + G * slot), F32) for slot, *_ in members], width
        )
        table_ref[CH : CH + 16, 128 * t : 128 * (t + 1)] = jnp.concatenate(
            [told, offs], 0
        ).astype(BF16)
        code = told[7:8]
        index = jnp.where(code < 0.0, code + MID, code + (MID - 1.0)) + base[0:1]
        key = jnp.where(code == 0.0, -5.0, index)
        column = jnp.broadcast_to(key, (128, 128)).T.astype(jnp.int32)
        key_ref[128 * t : 128 * (t + 1), :] = jnp.concatenate([column, column], 1)


def silu_parts(z):
    s = 0.5 * jnp.tanh(0.5 * z) + 0.5
    h = z * s
    return h, s + h * (1.0 - s)


def stack_high_low(x):
    return jnp.concatenate(high_low(x), 0).astype(BF16)


def span(b):
    return slice(BL * b, BL * (b + 1))


def pair_rows(ref, b):
    return jnp.concatenate([ref[2 * b], ref[2 * b + 1]], 1)


def twice_across(ref):
    x = ref[...].astype(F32).T
    return jnp.concatenate([x, x], 1).astype(BF16)


def prepare(r):
    r.own_table[...] = jnp.zeros_like(r.own_table)
    feat = r.feat[...].astype(F32).T
    r.own_table[0:CH, 0:A] = feat.astype(BF16)
    none = jnp.zeros((4, A), F32)
    pos = jnp.concatenate([none, r.pos[...].astype(F32), none, none, none[:1]], 0)
    r.own_table[CH : CH + 16, 0:A] = pos.astype(BF16)
    r.first_t[...] = twice_across(r.first)
    r.second_t[...] = twice_across(r.second)
    r.third_t[...] = twice_across(r.third)
    mix = r.mix[...]
    r.mix_t[...] = mix.astype(F32).T.astype(BF16)
    r.mix_two[...] = jnp.concatenate([mix, mix], 1)
    head = jnp.broadcast_to(r.head[...].astype(F32), (128, 128)).T
    r.head_t[...] = jnp.concatenate([head] * 4, 1)
    kinds = r.species[...]
    base = jnp.zeros((1, A), F32)
    for k in range(SPECIES):
        base = base + jnp.where(kinds == k, r.shift[k], 0.0)
    r.base[...] = base
    count = r.count[0, 0, 0]

    for b in range(STEPS):
        source = pair_rows(r.source, b)
        target = pair_rows(r.target, b)
        live = 2 * b + (iota((1, BL), 1) >= PB).astype(jnp.int32) < count
        target = jnp.where(live, target, -1)
        atoms = iota((AP, BL), 0)
        pick_own = (atoms == source).astype(BF16)
        pick_target = (atoms == target).astype(BF16)
        r.from_own[b] = pick_own
        r.to_own[b, 0:AP, :] = pick_target
        r.to_own[b, AP : 2 * AP, :] = pick_target
        across = iota((PB, AP), 1)
        for half in range(2):
            part = jnp.broadcast_to(target[:, PB * half : PB * (half + 1)], (PB, PB))
            column = part.astype(F32).T.astype(jnp.int32)
            pick = (across == jnp.concatenate([column] * 4, 1)).astype(BF16)
            r.by_pair[512 * b + PB * half : 512 * b + PB * (half + 1), :] = pick
            r.by_pair[512 * b + BL + PB * half : 512 * b + BL + PB * (half + 1), :] = pick
        near = dot(r.own_table[...], pick_own)
        here = dot(r.own_table[CH : CH + 16, :], pick_target)
        r.near[:, span(b)] = jnp.concatenate([near[:CH], near[CH : CH + 8] - here[:8]], 0)


def gather(r, half):
    rows = slice(HALF * half, HALF * (half + 1))
    for b in range(STEPS):
        lanes = span(b)
        pick_ghost = (r.keys[rows, :] == pair_rows(r.source, b)).astype(BF16)
        r.from_ghost[b, rows, :] = pick_ghost
        found = dot(r.table[:, rows], pick_ghost)
        feats = r.near[:CH, lanes] + found[:CH]
        place = r.near[CH : CH + 8, lanes] + found[CH : CH + 8] + SIDE * found[CH + 8 : CH + 16]
        if half == NEAR:
            r.near[:CH, lanes] = feats
            r.near[CH : CH + 8, lanes] = place
        else:
            r.feats[:, lanes] = feats * SCALE
            r.geom[:, lanes] = place


def harmonics_of(x, y, z):
    return [
        ROOT3 * x * y,
        ROOT3 * y * z,
        0.5 * (2.0 * z * z - x * x - y * y),
        ROOT3 * x * z,
        0.5 * ROOT3 * (x * x - y * y),
    ]


def radial(r):
    v = r.geom[4:7, :]
    q = v[0:1] * v[0:1] + v[1:2] * v[1:2] + v[2:3] * v[2:3]
    keep = jnp.maximum(1.0 - q / CUT, 0.0)
    envelope = keep * keep
    d_envelope = keep * (-2.0 / CUT)
    centers = iota((NRB, NP), 0).astype(F32) * (CUT / (NRB - 1))
    away = q - centers
    bump = jnp.exp(-(away * away) / CUT)
    basis = bump * envelope
    d_basis = bump * (d_envelope - (2.0 / CUT) * away * envelope)
    z = dot(r.first_t[...], jnp.concatenate([stack_high_low(basis), stack_high_low(d_basis)], 1))
    h, slope = silu_parts(z[:, :NP])
    d = slope * z[:, NP:]
    z = dot(r.second_t[...], jnp.concatenate([stack_high_low(h), stack_high_low(d)], 1))
    h, slope = silu_parts(z[:, :NP])
    d = slope * z[:, NP:]
    r.hidden[0] = stack_high_low(h)
    r.hidden[1] = stack_high_low(d)


CHUNKS = ((0, 4), (4, 9))


def scatter(r):
    v = r.geom[4:7, :]
    ux, uy, uz = 0.5 * v[0:1], 0.5 * v[1:2], 0.5 * v[2:3]
    harmonics = [None, ux, uy, uz] + harmonics_of(ux, uy, uz)
    for first, last in CHUNKS:
        for b in range(STEPS):
            lanes = slice(BL * b, BL * (b + 1))
            for i in range(first, last):
                order = 0 if i == 0 else (1 if i < 4 else 2)
                part = slice(CH * order, CH * (order + 1))
                if i in (0, 1, 4):
                    z = dot(r.third_t[part, :], r.hidden[0, :, lanes])
                    r.radial[b, part, :] = z * r.feats[:, lanes]
                term = r.radial[b, part, :]
                if i:
                    term = term * harmonics[i][:, lanes]
                high, low = high_low(term)
                row = CH * i
                r.terms[row : row + CH, 512 * b : 512 * b + BL] = high.astype(BF16)
                r.terms[row : row + CH, 512 * b + BL : 512 * b + 512] = low.astype(BF16)
        rows = slice(CH * first, CH * last)
        r.moments[rows, :] = dot(r.terms[rows, :], r.by_pair[...])


def readout(r):
    def moment(i):
        return r.moments[CH * i : CH * (i + 1), :]

    squares = []
    for low, high in ((1, 4), (4, 9)):
        total = moment(low) * moment(low)
        for i in range(low + 1, high):
            total = total + moment(i) * moment(i)
        squares.append(total)
    invariants = jnp.concatenate([moment(0)] + squares, 0)
    high, low = high_low(invariants)
    mix_t = r.mix_t[...]
    mixed = dot(mix_t, high.astype(BF16)) + dot(mix_t, low.astype(BF16))
    head = r.head_t[...]
    h, slope = silu_parts(mixed)
    d_mixed = stack_high_low(head * slope)
    d_inv = dot(r.mix_two[...], d_mixed)
    for i in range(9):
        order = 0 if i == 0 else (1 if i < 4 else 2)
        grad = d_inv[CH * order : CH * (order + 1)]
        if order:
            grad = 2.0 * moment(i) * grad
        high, low = high_low(grad)
        r.grads[CH * i : CH * (i + 1), 0:AP] = high.astype(BF16)
        r.grads[CH * i : CH * (i + 1), AP : 2 * AP] = low.astype(BF16)
    r.out[0] = jnp.sum(head * h, axis=0, keepdims=True)[:, :A] + r.base[...]


def pulls(r):
    for b in range(STEPS):
        d = dot(r.third_t[...], r.hidden[1, :, span(b)])
        r.back[b] = dot(r.grads[...], r.to_own[b])
        v = r.geom[4:7, span(b)]
        along, across = [], []
        for i in range(9):
            order = 0 if i == 0 else (1 if i < 4 else 2)
            part = slice(CH * order, CH * (order + 1))
            grad = r.back[b, CH * i : CH * (i + 1), :]
            if order:
                along.append(jnp.sum(r.radial[b, part, :] * grad, axis=0, keepdims=True))
            slope = d[part] * r.feats[:, span(b)]
            across.append(jnp.sum(slope * grad, axis=0, keepdims=True))
        x, y, z = 0.5 * v[0:1], 0.5 * v[1:2], 0.5 * v[2:3]
        ax, ay, az, b0, b1, b2, b3, b4 = along
        dq = across[0] + x * across[1] + y * across[2] + z * across[3]
        for harmonic, c in zip(harmonics_of(x, y, z), across[4:]):
            dq = dq + harmonic * c
        gx = ax + ROOT3 * (y * b0 + z * b3 + x * b4) - x * b2
        gy = ay + ROOT3 * (x * b0 + z * b1 - y * b4) - y * b2
        gz = az + ROOT3 * (y * b1 + x * b3) + 2.0 * z * b2
        px = 0.5 * gx + 2.0 * dq * v[0:1]
        py = 0.5 * gy + 2.0 * dq * v[1:2]
        pz = 0.5 * gz + 2.0 * dq * v[2:3]
        pull = jnp.concatenate([px, py, pz, jnp.zeros((5, BL), F32)], 0)
        r.pull[b] = stack_high_low(pull)


def spread(pull_ref, pick):
    total = None
    for b in range(STEPS):
        part = dot(pull_ref[b], pick(b), NT)
        total = part if total is None else total + part
    return total[:8] + total[8:]


def give_ghosts(r, half):
    rows = slice(HALF * half, HALF * (half + 1))
    r.ghost[:, rows] = -spread(r.pull, lambda b: r.from_ghost[b, rows, :])


def own_forces(r):
    return spread(r.pull, lambda b: r.to_own[b, 0:AP, :] - r.from_own[b])


class Refs:
    def __init__(self, names, refs):
        for name, ref in zip(names, refs, strict=True):
            setattr(self, name, ref)


LOADS = {
    "pos": ((3, A), BF16),
    "feat": ((A, CH), BF16),
    "list": ((1, G), jnp.int32),
    "source": ((NB, 1, PB), jnp.int32),
    "target": ((NB, 1, PB), jnp.int32),
    "first": ((NRB, RH), BF16),
    "second": ((RH, RH), BF16),
    "third": ((RH, 3 * CH), BF16),
    "mix": ((3 * CH, CH), BF16),
    "head": ((1, CH), BF16),
    "species": ((1, A), jnp.int32),
    "count": ((1, 1, 1), jnp.int32),
    "shift": ((SPECIES,), F32),
}
EARLY = ("pos", "list", "feat")
WORK = {
    "first_t": ((RH, 2 * NRB), BF16),
    "second_t": ((RH, 2 * RH), BF16),
    "third_t": ((3 * CH, 2 * RH), BF16),
    "mix_t": ((CH, 3 * CH), BF16),
    "mix_two": ((3 * CH, 2 * CH), BF16),
    "head_t": ((CH, AP), F32),
    "base": ((1, A), F32),
    "upper": ((A, A), BF16),
    "own_table": ((CH + 16, AP), BF16),
    "table": ((CH + 16, GT), BF16),
    "keys": ((GT, BL), jnp.int32),
    "from_own": ((STEPS, AP, BL), BF16),
    "from_ghost": ((STEPS, GT, BL), BF16),
    "to_own": ((STEPS, 2 * AP, BL), BF16),
    "by_pair": ((STEPS * 2 * BL, AP), BF16),
    "near": ((CH + 8, NP), F32),
    "feats": ((CH, NP), F32),
    "geom": ((8, NP), F32),
    "hidden": ((2, 2 * RH, NP), BF16),
    "radial": ((STEPS, 3 * CH, BL), F32),
    "terms": ((9 * CH, STEPS * 2 * BL), BF16),
    "moments": ((9 * CH, AP), F32),
    "grads": ((9 * CH, 2 * AP), BF16),
    "back": ((STEPS, 9 * CH, BL), F32),
    "pull": ((STEPS, 16, BL), BF16),
    "ghost": ((8, GT), F32),
    "pick": ((GT, A), BF16),
    "sent": ((SENT, CH), BF16),
    "got": ((SENT, CH), BF16),
    "returned": ((26, 4, 128), F32),
}
INPUTS = ["hbm_" + name for name in LOADS]
NAMES = INPUTS + ["out"] + list(LOADS) + list(WORK)
NAMES += ["load_sem", "send_sem", "recv_sem", "back_send_sem", "back_recv_sem"]


def kernel(*refs):
    r = Refs(NAMES, refs)
    at = neighbours()
    barrier = enter(at)
    loads = {}
    for i, name in enumerate(LOADS):
        loads[name] = pltpu.make_async_copy(
            getattr(r, "hbm_" + name), getattr(r, name), r.load_sem.at[i]
        )
        if name in EARLY:
            loads[name].start()
    for name in LOADS:
        if name not in EARLY:
            loads[name].start()
    r.upper[...] = (iota((A, A), 0) <= iota((A, A), 1)).astype(BF16)
    for name in EARLY:
        loads.pop(name).wait()
    copies = {}

    def send(half):
        if half == FAR:
            pl.semaphore_wait(barrier, 26)
        for i, (slot, rows, row, lane) in ORDER:
            if lane // HALF != half:
                continue
            copies[i] = pltpu.make_async_remote_copy(
                src_ref=r.sent.at[row : row + rows, :],
                dst_ref=r.got.at[row : row + rows, :],
                send_sem=r.send_sem.at[i],
                recv_sem=r.recv_sem.at[i],
                device_id=at(slot, -1),
                device_id_type=MESH,
            )
            copies[i].start()

    choose(r.pos, r.feat, r.list, r.upper, r.pick, r.sent, send)
    for copy in loads.values():
        copy.wait()
    prepare(r)
    for half in (NEAR, FAR):
        for members in tiles_of(half).values():
            for i, _ in members:
                copies[i].wait_recv()
        ghost_table(r.got, r.table, r.keys, half)
        gather(r, half)
    radial(r)
    scatter(r)
    readout(r)
    pulls(r)
    returns = {}
    for half in (FAR, NEAR):
        give_ghosts(r, half)
        for i, (slot, rows, _, lane) in ORDER:
            if lane // HALF != half:
                continue
            start = lane // 128 * 128
            returns[i] = pltpu.make_async_remote_copy(
                src_ref=r.ghost.at[0:4, start : start + 128],
                dst_ref=r.returned.at[i],
                send_sem=r.back_send_sem.at[i],
                recv_sem=r.back_recv_sem.at[i],
                device_id=at(slot, 1),
                device_id_type=MESH,
            )
            returns[i].start()
    total = own_forces(r)[:4, :A]
    for copy in copies.values():
        copy.wait_send()
    for half in (NEAR, FAR):
        tiles = []
        for members in tiles_of(half).values():
            for i, _ in members:
                returns[i].wait_recv()
            got = [r.returned[i] for i, _ in members]
            tiles.append(group_lanes(got, 128 // len(members)))
        got = stack_high_low(jnp.concatenate(tiles, 1))
        sums = dot(got, r.pick[HALF * half : HALF * (half + 1), :])
        total = total + sums[:4] + sums[4:]
    for axis in range(3):
        r.out[axis + 1] = total[axis : axis + 1]
    for copy in returns.values():
        copy.wait_send()


def split_kernel(both_ref, energy_ref, force_ref, sem):
    first = pltpu.make_async_copy(both_ref.at[0:1], energy_ref, sem.at[0])
    second = pltpu.make_async_copy(both_ref.at[1:4], force_ref, sem.at[1])
    first.start()
    second.start()
    first.wait()
    second.wait()


def vmem():
    return pl.BlockSpec(memory_space=pltpu.VMEM)


def shape(dims, kind=F32):
    return jax.ShapeDtypeStruct(dims, kind)


def shards(
    positions,
    features,
    species,
    species_shift,
    send_index,
    pair_target,
    pair_source,
    block_count,
    radial_first,
    radial_second,
    radial_third,
    invariant_mix,
    energy_head,
):
    both = pl.pallas_call(
        kernel,
        out_shape=pltpu.VMEM((4, 1, A), F32),
        in_specs=[pl.BlockSpec(memory_space=pl.ANY)] * len(LOADS),
        out_specs=vmem(),
        scratch_shapes=[
            (pltpu.SMEM if name in ("count", "shift") else pltpu.VMEM)(*spec)
            for name, spec in LOADS.items()
        ]
        + [pltpu.VMEM(*spec) for spec in WORK.values()]
        + [pltpu.SemaphoreType.DMA((len(LOADS),))]
        + [pltpu.SemaphoreType.DMA((26,))] * 4,
        compiler_params=pltpu.CompilerParams(
            collective_id=0, has_side_effects=True, vmem_limit_bytes=56 * 2**20
        ),
        name="layer",
    )(
        positions.reshape(3, A),
        jnp.swapaxes(features, 3, 4).reshape(A, CH),
        send_index.reshape(1, G),
        pair_source.reshape(NB, 1, PB),
        pair_target.reshape(NB, 1, PB),
        radial_first,
        radial_second,
        radial_third,
        invariant_mix,
        energy_head.reshape(1, CH),
        species.reshape(1, A),
        block_count,
        species_shift,
    )
    energies, forces = pl.pallas_call(
        split_kernel,
        out_shape=(shape((1, 1, A)), shape((3, 1, A))),
        in_specs=[vmem()],
        out_specs=(pl.BlockSpec(memory_space=pl.ANY),) * 2,
        scratch_shapes=[pltpu.SemaphoreType.DMA((2,))],
        compiler_params=pltpu.CompilerParams(vmem_limit_bytes=2**20),
        name="split",
    )(both)
    return (energies.reshape(1, 1, 1, A), forces.reshape(1, 1, 1, 3, A))


def solution(mesh):
    split = ("gx", "gy", "gz")
    return jax.shard_map(
        shards,
        mesh=mesh,
        in_specs=(
            P(*split, None, None),
            P(*split, None, None),
            P(*split, None),
            P(),
            P(*split, None),
            P(*split, None, None),
            P(*split, None, None),
            P(*split),
            P(),
            P(),
            P(),
            P(),
            P(),
        ),
        out_specs=(P(*split, None), P(*split, None, None)),
        check_vma=False,
    )
```
